32 devices in a mesh: section: 2 (over x), rep: 16 (over z, y, core).
Axes of the slice: x: 2, y: 2, z: 4, core: 2. Of those that a mesh axis runs over, the one named last changes fastest.
Arguments:
- layer_in: bfloat16 [2, 64, 4096], P('section', 'rep'), may hold values from -6 to 6
- next_in: bfloat16 [2, 64, 4096], P('section', 'rep'), may hold values from -6 to 6
- returned: bfloat16 [2, 128, 4096], P('section', 'rep'), may hold values from -6 to 6
- norm_gain: float32 [2, 4096], P('section'), may hold values from 0.25 to 1.75
- gate_weight: bfloat16 [2, 4096, 14336], P('section', None, 'rep'), may hold values from -0.09375 to 0.09375
- up_weight: bfloat16 [2, 4096, 14336], P('section', None, 'rep'), may hold values from -0.09375 to 0.09375
- down_weight: bfloat16 [2, 14336, 4096], P('section', 'rep'), may hold values from -0.046875 to 0.046875
- wiring: int32 [2, 16, 16], P('section'), may hold values from 0 to 2, as said below
Outputs:
- forwarded: bfloat16 [2, 128, 4096], P('section', 'rep')
- input_grad: bfloat16 [2, 64, 4096], P('section', 'rep')
- next_out: bfloat16 [2, 64, 4096], P('section', 'rep')
The draws below stay inside these ranges and needn't reach their ends.
Inputs may be any that keep to these rules, and one draw needn't show every extreme that they name: For every position p and row group r the entries wiring[p, r, :] sum to 2. For every position p and receiver j the column wiring[p, :, j] sums to at most 4, and in every position some column sums to exactly 4. In every position some row group sends all its 2 blocks to one receiver, and some receiver gets none.
All inputs are finite; a program needn't handle non-finite values.
Results may differ from the reference program's by a relative error of at most 0.035.
Values may be sent and summed in bfloat16 or wider, within the bound.
A program may use at most 128 MiB of HBM per device.

```python
import jax
import jax.numpy as jnp
from jax import lax

D = 4096
FF = 14336
ROWS = 4
BLK = 2
POSITIONS = 2
NB = 2
CAP = 4
TOKENS = 64
SLOTS = 128
N_SECTION = 2
N_REP = 16


def draw_section(section_key):
    key_pair, key_shift, key_shuffle, key_row = jax.random.split(section_key, 4)
    half_count = N_REP // 2
    pairing = jax.random.permutation(key_pair, N_REP)
    load_shift = jax.random.randint(key_shift, (half_count,), 0, NB + 1).astype(jnp.int32)
    load_shift = load_shift.at[0].set(NB)
    receiver_loads = jnp.zeros((N_REP,), jnp.int32)
    receiver_loads = receiver_loads.at[pairing[:half_count]].set(NB + load_shift)
    receiver_loads = receiver_loads.at[pairing[half_count:]].set(NB - load_shift)
    rest_loads = receiver_loads.at[pairing[0]].add(-NB)
    rest_dest = jnp.repeat(jnp.arange(N_REP, dtype=jnp.int32), rest_loads, total_repeat_length=(N_REP - 1) * NB)
    rest_dest = jax.random.permutation(key_shuffle, rest_dest)
    full_row = jnp.full((NB,), pairing[0], jnp.int32)
    destinations = jnp.concatenate([full_row, rest_dest]).astype(jnp.int32)
    per_sender = destinations.reshape(N_REP, NB)
    row_shift = jax.random.randint(key_row, (), 0, N_REP).astype(jnp.int32)
    per_sender = jnp.roll(per_sender, row_shift, axis=0)
    member_ids = jnp.arange(N_REP, dtype=jnp.int32)
    return jnp.sum((per_sender[:, :, None] == member_ids[None, None, :]).astype(jnp.int32), axis=1).astype(jnp.int32)


def draw_wiring(key, part):
    section_keys = jax.random.split(key, N_SECTION)
    return jax.vmap(draw_section)(section_keys)


def block_levels(rng, dims, shards, least, top_value):
    loudness, own = 1.0, jax.random.fold_in(rng, 6)
    for position, shards_of in shards:
        draws = jnp.exp(jax.random.uniform(jax.random.fold_in(own, position), (shards_of,), jnp.float32, least / len(shards), top_value / len(shards)))
        loudness = loudness * jnp.repeat(draws, dims[position] // shards_of).reshape([-1 if axis == position else 1 for axis in range(len(dims))])
    return loudness


def gaussian(rng, shape, deviation, bound, cuts=(), kind=jnp.bfloat16):
    drawn = deviation * jax.random.normal(rng, shape, jnp.float32)
    if cuts:
        drawn = drawn * block_levels(rng, shape, cuts, -0.22, 0.18)
    return jnp.clip(drawn, -bound, bound).astype(kind)


def setup_inputs(seed: int = 0) -> dict:
    splits = jax.random.split(jax.random.key(seed), 9)
    return {
        "layer_in": gaussian(splits[0], (POSITIONS, TOKENS, D), 1.0, 6.0, ((0, 2), (1, 16))),
        "next_in": gaussian(splits[1], (POSITIONS, TOKENS, D), 1.0, 6.0, ((0, 2), (1, 16))),
        "returned": gaussian(splits[2], (POSITIONS, SLOTS, D), 1.0, 6.0, ((0, 2), (1, 16))),
        "norm_gain": jnp.clip(1.0 + 0.15 * jax.random.normal(splits[3], (POSITIONS, D), jnp.float32), 0.25, 1.75),
        "gate_weight": gaussian(splits[4], (POSITIONS, D, FF), D ** -0.5, 0.09375, ((0, 2), (2, 16))),
        "up_weight": gaussian(splits[5], (POSITIONS, D, FF), D ** -0.5, 0.09375, ((0, 2), (2, 16))),
        "down_weight": gaussian(splits[6], (POSITIONS, FF, D), FF ** -0.5, 0.046875, ((0, 2), (1, 16))),
        "wiring": draw_wiring(jax.random.fold_in(splits[8], 71), 0),
    }


epsilon = 1e-05
step_rate = 0.5

def route_tables(wiring_section, replicas, blocks_dev, capacity):
    counts = wiring_section.astype(jnp.int32)
    row_total = jnp.cumsum(counts, axis=1).astype(jnp.int32)
    column_total = jnp.cumsum(counts, axis=0).astype(jnp.int32)
    row_start = (row_total - counts).astype(jnp.int32)
    column_start = (column_total - counts).astype(jnp.int32)
    slot_ids = jnp.arange(capacity, dtype=jnp.int32)
    block_ids = jnp.arange(blocks_dev, dtype=jnp.int32)
    member_ids = jnp.arange(replicas, dtype=jnp.int32)
    sender = lax.optimization_barrier(jnp.sum((column_total.T[:, :, None] <= slot_ids[None, None, :]).astype(jnp.int32), axis=1)).astype(jnp.int32)
    slot_live = slot_ids[None, :] < column_total[replicas - 1][:, None]
    sender = jnp.minimum(sender, replicas - 1)
    within = slot_ids[None, :] - column_start[sender, member_ids[:, None]]
    within = jnp.where(slot_live, within, 0).astype(jnp.int32)
    local_source = (sender * blocks_dev + within).astype(jnp.int32)
    global_source = (sender * blocks_dev + row_start[sender, member_ids[:, None]] + within).astype(jnp.int32)
    target_member = lax.optimization_barrier(jnp.sum((row_total[:, None, :] <= block_ids[None, :, None]).astype(jnp.int32), axis=2)).astype(jnp.int32)
    target_member = jnp.minimum(target_member, replicas - 1)
    block_offset = (block_ids[None, :] - row_start[member_ids[:, None], target_member]).astype(jnp.int32)
    global_target = (target_member * capacity + column_start[member_ids[:, None], target_member] + block_offset).astype(jnp.int32)
    local_target = (target_member * blocks_dev + block_offset).astype(jnp.int32)
    return (counts, row_start, column_start, slot_live, local_source, global_source, global_target, local_target)

def down_product(operands):
    return jnp.dot(operands[0], operands[1], preferred_element_type=jnp.float32)

def normalize(layer_rows, gain_row):
    values = layer_rows.astype(jnp.float32)
    row_scale = lax.rsqrt(lax.optimization_barrier(jnp.mean(values * values, axis=1, keepdims=True)) + epsilon)
    normed = (values * row_scale * gain_row[None, :]).astype(jnp.bfloat16)
    return (values, row_scale, normed)

def down_sum(hidden, down_weight, values):
    shard_units = FF // N_REP
    hidden_parts = hidden.reshape(TOKENS, N_REP, shard_units).transpose(1, 0, 2)
    down_parts = down_weight.reshape(N_REP, shard_units, D)
    partial_value = lax.map(down_product, (hidden_parts, down_parts))
    owner_term = jnp.eye(N_REP, dtype=jnp.float32)[:, :, None, None] * values.reshape(1, N_REP, ROWS, D)
    shard_terms = (partial_value.reshape(N_REP, N_REP, ROWS, D) + owner_term).astype(jnp.bfloat16)
    shard_terms = lax.optimization_barrier(shard_terms)
    return lax.optimization_barrier(jnp.sum(shard_terms.astype(jnp.float32), axis=0)).reshape(TOKENS, D).astype(jnp.bfloat16)

def section_forward(layer_rows, gain_row, gate_weight, up_weight, down_weight):
    values, row_scale, normed = normalize(layer_rows, gain_row)
    gate_act = jnp.dot(normed, gate_weight, preferred_element_type=jnp.float32)
    up_act = jnp.dot(normed, up_weight, preferred_element_type=jnp.float32)
    hidden = (jax.nn.silu(gate_act) * up_act).astype(jnp.bfloat16)
    layer_out = down_sum(hidden, down_weight, values)
    return (layer_out, values, row_scale, normed, gate_act, up_act, hidden)

def next_forward(layer_rows, gain_row, own_gate, mate_gate, own_up, mate_up, averaged_down):
    values, row_scale, normed = normalize(layer_rows, gain_row)
    gate_act = 0.5 * (jnp.dot(normed, own_gate, preferred_element_type=jnp.float32) + jnp.dot(normed, mate_gate, preferred_element_type=jnp.float32))
    up_act = 0.5 * (jnp.dot(normed, own_up, preferred_element_type=jnp.float32) + jnp.dot(normed, mate_up, preferred_element_type=jnp.float32))
    hidden = (jax.nn.silu(gate_act) * up_act).astype(jnp.bfloat16)
    return down_sum(hidden, averaged_down, values)

def backward_term(operands):
    dgate_part, dup_part, gate_part, up_part = operands
    contract = (((1,), (1,)), ((), ()))
    first = lax.dot_general(dgate_part, gate_part, contract, preferred_element_type=jnp.float32)
    second = lax.dot_general(dup_part, up_part, contract, preferred_element_type=jnp.float32)
    return (first + second).astype(jnp.bfloat16)

def section_backward(cotangent, values, row_scale, gain_row, normed, gate_act, up_act, hidden, gate_weight, up_weight, down_weight):
    dhidden = jnp.dot(cotangent, down_weight.T, preferred_element_type=jnp.float32)
    sigmoid_gate = jax.nn.sigmoid(gate_act)
    silu_gate = gate_act * sigmoid_gate
    grad_gate_act = (dhidden * up_act * sigmoid_gate * (1.0 + gate_act * (1.0 - sigmoid_gate))).astype(jnp.bfloat16)
    grad_up_act = (dhidden * silu_gate).astype(jnp.bfloat16)
    shard_units = FF // N_REP
    gate_parts = gate_weight.reshape(D, N_REP, shard_units).transpose(1, 0, 2)
    up_parts = up_weight.reshape(D, N_REP, shard_units).transpose(1, 0, 2)
    dgate_parts = grad_gate_act.reshape(TOKENS, N_REP, shard_units).transpose(1, 0, 2)
    dup_parts = grad_up_act.reshape(TOKENS, N_REP, shard_units).transpose(1, 0, 2)
    dterms = lax.map(backward_term, (dgate_parts, dup_parts, gate_parts, up_parts))
    dterms = lax.optimization_barrier(dterms)
    dnormed = lax.optimization_barrier(jnp.sum(dterms.astype(jnp.float32), axis=0))
    scaled_grad = gain_row[None, :] * dnormed
    input_grad = (cotangent.astype(jnp.float32) + row_scale * scaled_grad - values * row_scale ** 3 * lax.optimization_barrier(jnp.mean(values * scaled_grad, axis=1, keepdims=True))).astype(jnp.bfloat16)
    grad_gate = jnp.dot(normed.T, grad_gate_act, preferred_element_type=jnp.float32)
    grad_up = jnp.dot(normed.T, grad_up_act, preferred_element_type=jnp.float32)
    grad_down = jnp.dot(hidden.T, cotangent, preferred_element_type=jnp.float32)
    return (input_grad, grad_gate, grad_up, grad_down)

def apply_update(weight, gradient):
    updated = (weight.astype(jnp.float32) - step_rate / TOKENS * gradient).astype(jnp.bfloat16)
    return lax.optimization_barrier(updated)

def reference(layer_in, next_in, returned, norm_gain, gate_weight, up_weight, down_weight, wiring):
    forwarded_list = [None] * N_SECTION
    input_grads = [None] * N_SECTION
    next_outs = [None] * N_SECTION
    half_count = N_SECTION // 2
    for section_index in range(half_count):
        members = (section_index, section_index + half_count)
        updated_sets = {}
        for place in members:
            following = (place + 1) % N_SECTION
            layer_out, values, row_scale, normed, gate_act, up_act, hidden = section_forward(layer_in[place], norm_gain[place], gate_weight[place], up_weight[place], down_weight[place])
            tables = route_tables(wiring[place], N_REP, NB, CAP)
            slot_live, global_source, global_target = (tables[3], tables[5], tables[6])
            out_blocks = layer_out.reshape(N_REP * NB, BLK, D)
            slot_blocks = jnp.take(out_blocks, global_source.reshape(-1), axis=0).reshape(N_REP, CAP, BLK, D)
            slot_blocks = jnp.where(slot_live[:, :, None, None], slot_blocks, jnp.zeros((), jnp.bfloat16))
            forwarded_list[following] = slot_blocks.reshape(SLOTS, D)
            later_slots = returned[following].reshape(N_REP * CAP, BLK, D)
            cotangent = jnp.take(later_slots, global_target.reshape(-1), axis=0).reshape(TOKENS, D)
            input_grad, grad_gate, grad_up, grad_down = section_backward(cotangent, values, row_scale, norm_gain[place], normed, gate_act, up_act, hidden, gate_weight[place], up_weight[place], down_weight[place])
            input_grads[place] = input_grad
            updated_sets[place] = (apply_update(gate_weight[place], grad_gate), apply_update(up_weight[place], grad_up), apply_update(down_weight[place], grad_down))
        for place in members:
            partner = (place + half_count) % N_SECTION
            own_set = updated_sets[place]
            mate_set = updated_sets[partner]
            averaged_down = ((own_set[2].astype(jnp.float32) + mate_set[2].astype(jnp.float32)) * 0.5).astype(jnp.bfloat16)
            next_outs[place] = next_forward(next_in[place], norm_gain[place], own_set[0], mate_set[0], own_set[1], mate_set[1], averaged_down)
    return (jnp.stack(forwarded_list), jnp.stack(input_grads), jnp.stack(next_outs))
```

```python
import jax
import jax.numpy as jnp
from jax import lax
from jax.sharding import PartitionSpec as P

BLK = 2
epsilon = 1e-05
step_rate = 0.5
F32 = jnp.float32
BF16 = jnp.bfloat16


def passed_along(value, by):
    peers = lax.axis_size("section")
    return lax.ppermute(value, "section", [(i, (i + by) % peers) for i in range(peers)])


def route_select(counts, replicas, blocks_dev, capacity):
    blocks = replicas * blocks_dev
    row_total = jnp.cumsum(counts, axis=1)
    column_start = jnp.cumsum(counts, axis=0) - counts
    row_start = row_total - counts
    block_ids = jnp.arange(blocks_dev, dtype=jnp.int32)
    inside = (block_ids[None, :, None] >= row_start[:, None, :]) & (
        block_ids[None, :, None] < row_total[:, None, :]
    )
    member_ids = jnp.arange(replicas, dtype=jnp.int32)
    slot = member_ids[None, None, :] * capacity + (
        column_start[:, None, :] + block_ids[None, :, None] - row_start[:, None, :]
    )
    target = jnp.sum(jnp.where(inside, slot, 0), axis=2).reshape(blocks)
    return target


def row_one_hot(target, slots):
    rows = jnp.arange(slots * BLK, dtype=jnp.int32)
    target_rows = (target[:, None] * BLK + jnp.arange(BLK, dtype=jnp.int32)[None, :]).reshape(-1)
    return (rows[:, None] == target_rows[None, :]).astype(BF16)


def mm(a, b):
    return jnp.dot(a, b, preferred_element_type=F32)


def mm_t(a, b):
    return lax.dot_general(a, b, (((1,), (1,)), ((), ())), preferred_element_type=F32)


def normalize(layer_rows, gain_row):
    values = layer_rows.astype(F32)
    row_scale = lax.rsqrt(jnp.mean(values * values, axis=1, keepdims=True) + epsilon)
    return values, row_scale, (values * row_scale * gain_row[None, :]).astype(BF16)


def low_rank(coefs, factors):
    high = coefs.astype(BF16)
    low = (coefs - high.astype(F32)).astype(BF16)
    return mm(jnp.concatenate((high, low), 1), jnp.concatenate((factors, factors), 0))


def scatter_terms(terms):
    got = lax.all_to_all(terms, "rep", split_axis=0, concat_axis=0, tiled=True)
    return jnp.sum(got.astype(F32), axis=0)


def per_device(layer_in, next_in, returned, norm_gain, gate_weight, up_weight, down_weight, wiring):
    replicas = lax.axis_size("rep")
    position = lax.axis_index("rep")
    partner_offset = lax.axis_size("section") // 2
    rows = layer_in.shape[1]
    features = layer_in.shape[2]
    blocks_dev = rows // BLK
    slot_rows = returned.shape[1]
    capacity = slot_rows // BLK
    tokens = rows * replicas
    gain = norm_gain[0]
    gate, up, down = gate_weight[0], up_weight[0], down_weight[0]
    factor = step_rate / tokens

    values, row_scale, normed_own = normalize(layer_in[0], gain)
    next_values, _, next_own = normalize(next_in[0], gain)
    next_mate = passed_along(next_own, partner_offset)
    later = passed_along(returned[0], -1)
    packed = jnp.concatenate((normed_own, next_own, next_mate, later), 0)
    target = route_select(wiring[0], replicas, blocks_dev, capacity)
    select = row_one_hot(target, replicas * capacity)
    everything = lax.all_gather(packed, "rep", axis=0, tiled=False)
    normed = everything[:, :rows].reshape(tokens, features)
    nexts = jnp.concatenate(
        (
            everything[:, rows : 2 * rows].reshape(tokens, features),
            everything[:, 2 * rows : 3 * rows].reshape(tokens, features),
        ),
        0,
    )
    slots = everything[:, 3 * rows :].reshape(replicas * slot_rows, features)
    cotangent = lax.dot_general(
        select, slots, (((0,), (0,)), ((), ())), preferred_element_type=F32
    ).astype(BF16)

    lhs = jnp.concatenate((normed, nexts), 0)
    gate_all = mm(lhs, gate)
    up_all = mm(lhs, up)
    gate_act, up_act = gate_all[:tokens], up_all[:tokens]
    sigmoid = jax.nn.sigmoid(gate_act)
    silu = gate_act * sigmoid
    hidden = (silu * up_act).astype(BF16)
    dhidden = mm_t(cotangent, down)
    d_gate = (dhidden * up_act * sigmoid * (1.0 + gate_act * (1.0 - sigmoid))).astype(BF16)
    d_up = (dhidden * silu).astype(BF16)

    coefs = factor * mm_t(nexts, normed)
    next_gate = 0.5 * (gate_all[tokens:] - low_rank(coefs, d_gate))
    next_up = 0.5 * (up_all[tokens:] - low_rank(coefs, d_up))
    to_mate = jnp.stack((next_gate[tokens:], next_up[tokens:])).astype(BF16)
    from_mate = passed_along(to_mate, partner_offset).astype(F32)

    dterm = (mm_t(d_gate, gate) + mm_t(d_up, up)).astype(BF16)
    term = mm(hidden, down)
    own = lax.dynamic_slice_in_dim(term, position * rows, rows, 0) + values
    term = lax.dynamic_update_slice_in_dim(term, own, position * rows, 0).astype(BF16)
    slot_term = mm(select, term).astype(BF16)
    first = scatter_terms(
        jnp.concatenate(
            (
                slot_term.reshape(replicas, slot_rows, features),
                dterm.reshape(replicas, rows, features),
            ),
            1,
        )
    )

    gate_next = next_gate[:tokens] + from_mate[0]
    up_next = next_up[:tokens] + from_mate[1]
    hidden_own = (jax.nn.silu(gate_next) * up_next).astype(BF16)
    hidden_mate = passed_along(hidden_own, partner_offset)
    hidden_both = jnp.concatenate((hidden_own, hidden_mate), 0)
    down_coefs = factor * mm_t(hidden_both, hidden)
    term_next = (0.5 * (mm(hidden_both, down) - low_rank(down_coefs, cotangent))).astype(BF16)
    term_next = term_next.reshape(2, replicas, rows, features).transpose(1, 0, 2, 3)
    second = scatter_terms(term_next.reshape(replicas, 2 * rows, features))
    mate_sum = passed_along(second[rows:], partner_offset)
    next_out = (second[:rows] + mate_sum + next_values).astype(BF16)

    forwarded = passed_along(first[:slot_rows].astype(BF16), 1)
    dnormed = first[slot_rows:]
    scaled = gain[None, :] * dnormed
    cotangent_own = lax.dynamic_slice_in_dim(cotangent, position * rows, rows, 0)
    input_grad = (
        cotangent_own.astype(F32)
        + row_scale * scaled
        - values * row_scale**3 * jnp.mean(values * scaled, axis=1, keepdims=True)
    ).astype(BF16)
    return (forwarded[None], input_grad[None], next_out[None])


def solution(mesh):
    in_specs = (
        P("section", "rep", None),
        P("section", "rep", None),
        P("section", "rep", None),
        P("section", None),
        P("section", None, "rep"),
        P("section", None, "rep"),
        P("section", "rep", None),
        P("section", None, None),
    )
    out_specs = (P("section", "rep", None), P("section", "rep", None), P("section", "rep", None))
    return jax.shard_map(
        per_device, mesh=mesh, in_specs=in_specs, out_specs=out_specs, check_vma=False
    )
```

```python
import functools

import jax
import jax.numpy as jnp
from jax import lax
from jax.experimental import pallas as pl
from jax.experimental.pallas import tpu as pltpu
from jax.sharding import PartitionSpec as P

BLK = 2
epsilon = 1e-05
step_rate = 0.5
F32 = jnp.float32
BF16 = jnp.bfloat16


QUARTERS = 4
CORES = 2
DEPTH_Z = 4


def place(ny):
    me = lax.axis_index("rep")

    def index(z, y, core):
        return (z * ny + y) * CORES + core

    return me // (CORES * ny), (me // CORES) % ny, me % CORES, index


def greet(ny, z, y, core, index):
    barrier = pltpu.get_barrier_semaphore()
    peers = [index((z + d) % DEPTH_Z, y, core) for d in range(1, DEPTH_Z)]
    peers += [index(z, (y + d) % ny, core) for d in range(1, ny)]
    peers += [index(z, y, 1 - core)]
    for peer in peers:
        pl.semaphore_signal(
            barrier, inc=1, device_id={"rep": peer}, device_id_type=pl.DeviceIdType.MESH
        )
    pl.semaphore_wait(barrier, len(peers))


def remote(src, dst, send, recv, peer):
    return pltpu.make_async_remote_copy(
        src_ref=src,
        dst_ref=dst,
        send_sem=send,
        recv_sem=recv,
        device_id={"rep": peer},
        device_id_type=pl.DeviceIdType.MESH,
    )


def gather_kernel(ny, x_ref, out_ref, send, recv):
    z, y, core, index = place(ny)
    greet(ny, z, y, core, index)
    me = index(z, y, core)
    sibling = index(z, y, 1 - core)
    out_ref[me] = x_ref[...]
    started = []

    def push(shard, peer):
        copy = remote(
            out_ref.at[shard], out_ref.at[shard], send.at[len(started)], recv.at[shard], peer
        )
        copy.start()
        started.append(copy)

    def arrive(shard):
        remote(
            out_ref.at[shard], out_ref.at[shard], send.at[0], recv.at[shard], sibling
        ).wait_recv()

    z_order = [1, DEPTH_Z - 1] + list(range(2, DEPTH_Z - 1))
    for dz in z_order:
        push(me, index((z + dz) % DEPTH_Z, y, core))
    for dz in [0] + z_order:
        shard = index((z + dz) % DEPTH_Z, y, core)
        if dz:
            arrive(shard)
        for dy in range(1, ny):
            push(shard, index(z, (y + dy) % ny, core))
        push(shard, sibling)
    for dz in [0] + z_order:
        for dy in range(1, ny):
            shard = index((z + dz) % DEPTH_Z, (y + dy) % ny, core)
            arrive(shard)
            push(shard, sibling)
    for dz in [0] + z_order:
        for dy in range(ny):
            arrive(index((z + dz) % DEPTH_Z, (y + dy) % ny, 1 - core))
    for copy in started:
        copy.wait_send()


def gather_shards(shard):
    replicas = lax.axis_size("rep")
    ny = replicas // (CORES * DEPTH_Z)
    copies = DEPTH_Z - 1 + DEPTH_Z * ny + DEPTH_Z * (ny - 1)
    return pl.pallas_call(
        functools.partial(gather_kernel, ny),
        out_shape=jax.ShapeDtypeStruct((replicas,) + shard.shape, shard.dtype),
        in_specs=[pl.BlockSpec(memory_space=pltpu.VMEM)],
        out_specs=pl.BlockSpec(memory_space=pltpu.VMEM),
        scratch_shapes=[
            pltpu.SemaphoreType.DMA((copies,)),
            pltpu.SemaphoreType.DMA((replicas,)),
        ],
        compiler_params=pltpu.CompilerParams(
            collective_id=0, has_side_effects=True, vmem_limit_bytes=32 * 2**20
        ),
    )(shard)


def sum_kernel(
    ny, t_ref, out_ref, from_core, part, from_y, summed, from_z, send, recv_core, recv_y, recv_z
):
    z, y, core, index = place(ny)
    greet(ny, z, y, core, index)
    sibling = index(z, y, 1 - core)
    started = []

    def push(src, dst, recv, peer):
        copy = remote(src, dst, send.at[len(started)], recv, peer)
        copy.start()
        started.append(copy)
        return copy

    y_order = list(range(1, ny)) + [0]
    z_order = list(range(2, DEPTH_Z - 1)) + [1, DEPTH_Z - 1, 0]
    core_copies = {}
    for dy in y_order:
        yy = (y + dy) % ny
        core_copies[dy] = push(
            t_ref.at[1 - core, yy], from_core.at[yy], recv_core.at[dy], sibling
        )
    y_copies = []
    for dy in y_order[:-1]:
        yy = (y + dy) % ny
        core_copies[dy].wait_recv()
        part[dy - 1] = (t_ref[core, yy].astype(F32) + from_core[yy].astype(F32)).astype(BF16)
        y_copies.append(
            push(part.at[dy - 1], from_y.at[dy - 1], recv_y.at[dy - 1], index(z, yy, core))
        )
    core_copies[0].wait_recv()
    for copy in y_copies:
        copy.wait_recv()
    z_copies = []
    total = None
    for dz in z_order:
        zz = (z + dz) % DEPTH_Z
        total = t_ref[core, y, zz].astype(F32) + from_core[y, zz].astype(F32)
        for dy in range(1, ny):
            total = total + from_y[dy - 1, zz].astype(F32)
        if dz:
            summed[dz - 1] = total.astype(BF16)
            z_copies.append(
                push(
                    summed.at[dz - 1], from_z.at[dz - 1], recv_z.at[dz - 1], index(zz, y, core)
                )
            )
    out_ref[...] = total
    for dz, copy in zip(z_order, z_copies):
        copy.wait_recv()
        out_ref[...] += from_z[dz - 1].astype(F32)
    for copy in started:
        copy.wait_send()


def sum_shards(terms, collective_id):
    replicas, rows, features = terms.shape
    ny = replicas // (CORES * DEPTH_Z)
    width = features // QUARTERS
    tall = rows * QUARTERS
    laid = terms.reshape(DEPTH_Z, ny, CORES, rows, QUARTERS, width)
    laid = laid.transpose(2, 1, 0, 4, 3, 5).reshape(CORES, ny, DEPTH_Z, tall, width)
    copies = ny + ny - 1 + DEPTH_Z - 1
    total = pl.pallas_call(
        functools.partial(sum_kernel, ny),
        out_shape=jax.ShapeDtypeStruct((tall, width), F32),
        in_specs=[pl.BlockSpec(memory_space=pltpu.VMEM)],
        out_specs=pl.BlockSpec(memory_space=pltpu.VMEM),
        scratch_shapes=[
            pltpu.VMEM((ny, DEPTH_Z, tall, width), BF16),
            pltpu.VMEM((ny - 1, DEPTH_Z, tall, width), BF16),
            pltpu.VMEM((ny - 1, DEPTH_Z, tall, width), BF16),
            pltpu.VMEM((DEPTH_Z - 1, tall, width), BF16),
            pltpu.VMEM((DEPTH_Z - 1, tall, width), BF16),
            pltpu.SemaphoreType.DMA((copies,)),
            pltpu.SemaphoreType.DMA((ny,)),
            pltpu.SemaphoreType.DMA((ny - 1,)),
            pltpu.SemaphoreType.DMA((DEPTH_Z - 1,)),
        ],
        compiler_params=pltpu.CompilerParams(
            collective_id=collective_id, has_side_effects=True, vmem_limit_bytes=32 * 2**20
        ),
    )(laid)
    return total.reshape(QUARTERS, rows, width).transpose(1, 0, 2).reshape(rows, features)


def passed_along(value, by):
    peers = lax.axis_size("section")
    return lax.ppermute(value, "section", [(i, (i + by) % peers) for i in range(peers)])


def route_select(counts, replicas, blocks_dev, capacity):
    blocks = replicas * blocks_dev
    row_total = jnp.cumsum(counts, axis=1)
    column_start = jnp.cumsum(counts, axis=0) - counts
    row_start = row_total - counts
    block_ids = jnp.arange(blocks_dev, dtype=jnp.int32)
    inside = (block_ids[None, :, None] >= row_start[:, None, :]) & (
        block_ids[None, :, None] < row_total[:, None, :]
    )
    member_ids = jnp.arange(replicas, dtype=jnp.int32)
    slot = member_ids[None, None, :] * capacity + (
        column_start[:, None, :] + block_ids[None, :, None] - row_start[:, None, :]
    )
    target = jnp.sum(jnp.where(inside, slot, 0), axis=2).reshape(blocks)
    return target


def row_one_hot(target, slots):
    rows = jnp.arange(slots * BLK, dtype=jnp.int32)
    target_rows = (target[:, None] * BLK + jnp.arange(BLK, dtype=jnp.int32)[None, :]).reshape(-1)
    return (rows[:, None] == target_rows[None, :]).astype(BF16)


def mm(a, b):
    return jnp.dot(a, b, preferred_element_type=F32)


def mm_t(a, b):
    return lax.dot_general(a, b, (((1,), (1,)), ((), ())), preferred_element_type=F32)


def normalize(layer_rows, gain_row):
    values = layer_rows.astype(F32)
    row_scale = lax.rsqrt(jnp.mean(values * values, axis=1, keepdims=True) + epsilon)
    return values, row_scale, (values * row_scale * gain_row[None, :]).astype(BF16)


def low_rank(coefs, factors):
    high = coefs.astype(BF16)
    low = (coefs - high.astype(F32)).astype(BF16)
    return mm(jnp.concatenate((high, low), 1), jnp.concatenate((factors, factors), 0))


def per_device(layer_in, next_in, returned, norm_gain, gate_weight, up_weight, down_weight, wiring):
    replicas = lax.axis_size("rep")
    position = lax.axis_index("rep")
    partner_offset = lax.axis_size("section") // 2
    rows = layer_in.shape[1]
    features = layer_in.shape[2]
    blocks_dev = rows // BLK
    slot_rows = returned.shape[1]
    capacity = slot_rows // BLK
    tokens = rows * replicas
    gain = norm_gain[0]
    gate, up, down = gate_weight[0], up_weight[0], down_weight[0]
    factor = step_rate / tokens

    values, row_scale, normed_own = normalize(layer_in[0], gain)
    next_values, _, next_own = normalize(next_in[0], gain)
    next_mate = passed_along(next_own, partner_offset)
    later = passed_along(returned[0], -1)
    packed = jnp.concatenate((normed_own, next_own, next_mate, later), 0)
    target = route_select(wiring[0], replicas, blocks_dev, capacity)
    select = row_one_hot(target, replicas * capacity)
    groups = packed.shape[0] // rows
    width = features // QUARTERS
    shard = packed.reshape(groups, rows, QUARTERS, width).transpose(0, 2, 1, 3)
    everything = gather_shards(shard.reshape(groups * QUARTERS * rows, width))
    everything = everything.reshape(replicas, groups, QUARTERS, rows, width)
    everything = everything.transpose(0, 1, 3, 2, 4).reshape(replicas, groups * rows, features)
    normed = everything[:, :rows].reshape(tokens, features)
    nexts = jnp.concatenate(
        (
            everything[:, rows : 2 * rows].reshape(tokens, features),
            everything[:, 2 * rows : 3 * rows].reshape(tokens, features),
        ),
        0,
    )
    slots = everything[:, 3 * rows :].reshape(replicas * slot_rows, features)
    cotangent = lax.dot_general(
        select, slots, (((0,), (0,)), ((), ())), preferred_element_type=F32
    ).astype(BF16)

    lhs = jnp.concatenate((normed, nexts), 0)
    gate_all = mm(lhs, gate)
    up_all = mm(lhs, up)
    gate_act, up_act = gate_all[:tokens], up_all[:tokens]
    sigmoid = jax.nn.sigmoid(gate_act)
    silu = gate_act * sigmoid
    hidden = (silu * up_act).astype(BF16)
    dhidden = mm_t(cotangent, down)
    d_gate = (dhidden * up_act * sigmoid * (1.0 + gate_act * (1.0 - sigmoid))).astype(BF16)
    d_up = (dhidden * silu).astype(BF16)

    coefs = factor * mm_t(nexts, normed)
    next_gate = 0.5 * (gate_all[tokens:] - low_rank(coefs, d_gate))
    next_up = 0.5 * (up_all[tokens:] - low_rank(coefs, d_up))
    to_mate = jnp.stack((next_gate[tokens:], next_up[tokens:])).astype(BF16)
    from_mate = passed_along(to_mate, partner_offset).astype(F32)

    dterm = (mm_t(d_gate, gate) + mm_t(d_up, up)).astype(BF16)
    term = mm(hidden, down)
    own = lax.dynamic_slice_in_dim(term, position * rows, rows, 0) + values
    term = lax.dynamic_update_slice_in_dim(term, own, position * rows, 0).astype(BF16)
    slot_term = mm(select, term).astype(BF16)
    first = sum_shards(
        jnp.concatenate(
            (
                slot_term.reshape(replicas, slot_rows, features),
                dterm.reshape(replicas, rows, features),
            ),
            1,
        ),
        1,
    )

    gate_next = next_gate[:tokens] + from_mate[0]
    up_next = next_up[:tokens] + from_mate[1]
    hidden_own = (jax.nn.silu(gate_next) * up_next).astype(BF16)
    hidden_mate = passed_along(hidden_own, partner_offset)
    hidden_both = jnp.concatenate((hidden_own, hidden_mate), 0)
    down_coefs = factor * mm_t(hidden_both, hidden)
    term_next = (0.5 * (mm(hidden_both, down) - low_rank(down_coefs, cotangent))).astype(BF16)
    term_next = term_next.reshape(2, replicas, rows, features).transpose(1, 0, 2, 3)
    second = sum_shards(term_next.reshape(replicas, 2 * rows, features), 2)
    mate_sum = passed_along(second[rows:], partner_offset)
    next_out = (second[:rows] + mate_sum + next_values).astype(BF16)

    forwarded = passed_along(first[:slot_rows].astype(BF16), 1)
    dnormed = first[slot_rows:]
    scaled = gain[None, :] * dnormed
    cotangent_own = lax.dynamic_slice_in_dim(cotangent, position * rows, rows, 0)
    input_grad = (
        cotangent_own.astype(F32)
        + row_scale * scaled
        - values * row_scale**3 * jnp.mean(values * scaled, axis=1, keepdims=True)
    ).astype(BF16)
    return (forwarded[None], input_grad[None], next_out[None])


def solution(mesh):
    in_specs = (
        P("section", "rep", None),
        P("section", "rep", None),
        P("section", "rep", None),
        P("section", None),
        P("section", None, "rep"),
        P("section", None, "rep"),
        P("section", "rep", None),
        P("section", None, None),
    )
    out_specs = (P("section", "rep", None), P("section", "rep", None), P("section", "rep", None))
    return jax.shard_map(
        per_device, mesh=mesh, in_specs=in_specs, out_specs=out_specs, check_vma=False
    )
```

```python
import functools

import jax
import jax.numpy as jnp
from jax import lax
from jax.experimental import pallas as pl
from jax.experimental.pallas import tpu as pltpu
from jax.sharding import PartitionSpec as P

BLK = 2
epsilon = 1e-05
step_rate = 0.5
F32 = jnp.float32
BF16 = jnp.bfloat16


QUARTERS = 4
CORES = 2
DEPTH_Z = 4


def place(ny):
    me = lax.axis_index("rep")

    def index(z, y, core):
        return (z * ny + y) * CORES + core

    return me // (CORES * ny), (me // CORES) % ny, me % CORES, index


def greet(ny, z, y, core, index, across=()):
    barrier = pltpu.get_barrier_semaphore()
    peers = [{"rep": index((z + d) % DEPTH_Z, y, core)} for d in range(1, DEPTH_Z)]
    peers += [{"rep": index(z, (y + d) % ny, core)} for d in range(1, ny)]
    peers += [{"rep": index(z, y, 1 - core)}]
    peers += [{"section": section} for section in across]
    for peer in peers:
        pl.semaphore_signal(
            barrier, inc=1, device_id=peer, device_id_type=pl.DeviceIdType.MESH
        )
    pl.semaphore_wait(barrier, len(peers))


def remote(src, dst, send, recv, peer):
    return pltpu.make_async_remote_copy(
        src_ref=src,
        dst_ref=dst,
        send_sem=send,
        recv_sem=recv,
        device_id=peer if isinstance(peer, dict) else {"rep": peer},
        device_id_type=pl.DeviceIdType.MESH,
    )


def gather_kernel(ny, a_ref, b_ref, a_out, b_out, send, recv):
    z, y, core, index = place(ny)
    greet(ny, z, y, core, index)
    me = index(z, y, core)
    sibling = index(z, y, 1 - core)
    a_out[me] = a_ref[...]
    b_out[me] = b_ref[...]
    outs = (a_out, b_out)
    started = []

    def push(shard, peer):
        for k, out in enumerate(outs):
            copy = remote(
                out.at[shard], out.at[shard], send.at[len(started)], recv.at[k, shard], peer
            )
            copy.start()
            started.append(copy)

    def arrive(shard):
        for k, out in enumerate(outs):
            remote(
                out.at[shard], out.at[shard], send.at[0], recv.at[k, shard], sibling
            ).wait_recv()

    z_order = [1, DEPTH_Z - 1] + list(range(2, DEPTH_Z - 1))
    for dz in z_order:
        push(me, index((z + dz) % DEPTH_Z, y, core))
    for dz in [0] + z_order:
        shard = index((z + dz) % DEPTH_Z, y, core)
        if dz:
            arrive(shard)
        for dy in range(1, ny):
            push(shard, index(z, (y + dy) % ny, core))
        push(shard, sibling)
    for dz in [0] + z_order:
        for dy in range(1, ny):
            shard = index((z + dz) % DEPTH_Z, (y + dy) % ny, core)
            arrive(shard)
            push(shard, sibling)
    for dz in [0] + z_order:
        for dy in range(ny):
            arrive(index((z + dz) % DEPTH_Z, (y + dy) % ny, 1 - core))
    for copy in started:
        copy.wait_send()


def gather_shards(*shards):
    replicas = lax.axis_size("rep")
    ny = replicas // (CORES * DEPTH_Z)
    copies = len(shards) * (DEPTH_Z - 1 + DEPTH_Z * ny + DEPTH_Z * (ny - 1))
    vmem = pl.BlockSpec(memory_space=pltpu.VMEM)
    return pl.pallas_call(
        functools.partial(gather_kernel, ny),
        out_shape=[jax.ShapeDtypeStruct((replicas,) + v.shape, v.dtype) for v in shards],
        in_specs=[vmem] * len(shards),
        out_specs=[vmem] * len(shards),
        scratch_shapes=[
            pltpu.SemaphoreType.DMA((copies,)),
            pltpu.SemaphoreType.DMA((len(shards), replicas)),
        ],
        compiler_params=pltpu.CompilerParams(
            collective_id=0, has_side_effects=True, vmem_limit_bytes=32 * 2**20
        ),
    )(*shards)


def sum_kernel(ny, routed, *refs):
    kinds = routed + 3
    terms = refs[:kinds]
    mate_out, slots_out, rest_out = refs[kinds : kinds + 3]
    from_core, part, from_y, summed, from_z, mate_sum, slot_sum = refs[kinds + 3 : kinds + 10]
    send, recv_core, recv_y, recv_z, recv_x = refs[kinds + 10 :]
    z, y, core, index = place(ny)
    sections = lax.axis_size("section")
    section = lax.axis_index("section")
    mate = (section + sections // 2) % sections
    following = (section + 1) % sections
    before = (section + sections - 1) % sections
    greet(ny, z, y, core, index, (mate, following, before))
    sibling = index(z, y, 1 - core)
    started = []

    def push(src, dst, recv, peer):
        copy = remote(src, dst, send.at[len(started)], recv, peer)
        copy.start()
        started.append(copy)
        return copy

    y_order = list(range(1, ny)) + [0]
    z_order = list(range(2, DEPTH_Z - 1)) + [1, DEPTH_Z - 1, 0]
    core_copies, y_copies, z_copies, totals = {}, {}, {}, {}
    for k in range(kinds):
        for dy in y_order:
            yy = (y + dy) % ny
            core_copies[k, dy] = push(
                terms[k].at[1 - core, yy], from_core.at[k, yy], recv_core.at[k, dy], sibling
            )

    def to_y(k):
        for dy in y_order[:-1]:
            yy = (y + dy) % ny
            core_copies[k, dy].wait_recv()
            part[k, dy - 1] = (
                terms[k][core, yy].astype(F32) + from_core[k, yy].astype(F32)
            ).astype(BF16)
            y_copies[k, dy] = push(
                part.at[k, dy - 1],
                from_y.at[k, dy - 1],
                recv_y.at[k, dy - 1],
                index(z, yy, core),
            )

    def to_z(k):
        core_copies[k, 0].wait_recv()
        for dy in y_order[:-1]:
            y_copies[k, dy].wait_recv()
        for dz in z_order:
            zz = (z + dz) % DEPTH_Z
            total = terms[k][core, y, zz].astype(F32) + from_core[k, y, zz].astype(F32)
            for dy in range(1, ny):
                total = total + from_y[k, dy - 1, zz].astype(F32)
            if dz:
                summed[k, dz - 1] = total.astype(BF16)
                z_copies[k, dz] = push(
                    summed.at[k, dz - 1],
                    from_z.at[k, dz - 1],
                    recv_z.at[k, dz - 1],
                    index(zz, y, core),
                )
        totals[k] = total

    x_copies = []

    def finish(k):
        total = totals[k]
        for dz in z_order[:-1]:
            z_copies[k, dz].wait_recv()
            total = total + from_z[k, dz - 1].astype(F32)
        if k == 0:
            mate_sum[...] = total
            x_copies.append(push(mate_sum, mate_out, recv_x.at[0], {"section": mate}))
        elif k <= routed:
            slot_sum[k - 1] = total.astype(BF16)
            x_copies.append(
                push(
                    slot_sum.at[k - 1],
                    slots_out.at[k - 1],
                    recv_x.at[k],
                    {"section": following},
                )
            )
        else:
            rest_out[k - routed - 1] = total

    for k in range(kinds + 2):
        if k < kinds:
            to_y(k)
        if 1 <= k <= kinds:
            to_z(k - 1)
        if k >= 2:
            finish(k - 2)
    for copy in x_copies:
        copy.wait_recv()
    for copy in started:
        copy.wait_send()


def lay_terms(terms):
    replicas, rows, features = terms.shape
    ny = replicas // (CORES * DEPTH_Z)
    width = features // QUARTERS
    laid = terms.reshape(DEPTH_Z, ny, CORES, rows, QUARTERS, width)
    return laid.transpose(2, 1, 0, 4, 3, 5).reshape(CORES, ny, DEPTH_Z, rows * QUARTERS, width)


def lay_back(value, rows):
    tall, width = value.shape[-2:]
    value = value.reshape(-1, QUARTERS, rows, width).transpose(0, 2, 1, 3)
    return value.reshape(-1, rows, QUARTERS * width)


def sum_terms(mate_terms, slot_terms, d_terms, own_terms):
    laid = [lay_terms(v) for v in (mate_terms, *slot_terms, d_terms, own_terms)]
    _, ny, _, tall, width = laid[0].shape
    routed = len(slot_terms)
    kinds = len(laid)
    rows = mate_terms.shape[1]
    copies = kinds * (ny + ny - 1 + DEPTH_Z - 1) + 1 + routed
    vmem = pl.BlockSpec(memory_space=pltpu.VMEM)
    mate, slots, rest = pl.pallas_call(
        functools.partial(sum_kernel, ny, routed),
        out_shape=[
            jax.ShapeDtypeStruct((tall, width), F32),
            jax.ShapeDtypeStruct((routed, tall, width), BF16),
            jax.ShapeDtypeStruct((2, tall, width), F32),
        ],
        in_specs=[vmem] * kinds,
        out_specs=[vmem] * 3,
        scratch_shapes=[
            pltpu.VMEM((kinds, ny, DEPTH_Z, tall, width), BF16),
            pltpu.VMEM((kinds, ny - 1, DEPTH_Z, tall, width), BF16),
            pltpu.VMEM((kinds, ny - 1, DEPTH_Z, tall, width), BF16),
            pltpu.VMEM((kinds, DEPTH_Z - 1, tall, width), BF16),
            pltpu.VMEM((kinds, DEPTH_Z - 1, tall, width), BF16),
            pltpu.VMEM((tall, width), F32),
            pltpu.VMEM((routed, tall, width), BF16),
            pltpu.SemaphoreType.DMA((copies,)),
            pltpu.SemaphoreType.DMA((kinds, ny)),
            pltpu.SemaphoreType.DMA((kinds, ny - 1)),
            pltpu.SemaphoreType.DMA((kinds, DEPTH_Z - 1)),
            pltpu.SemaphoreType.DMA((1 + routed,)),
        ],
        compiler_params=pltpu.CompilerParams(
            collective_id=1, has_side_effects=True, vmem_limit_bytes=40 * 2**20
        ),
    )(*laid)
    rest = lay_back(rest, rows)
    return lay_back(mate, rows)[0], lay_back(slots, rows), rest[0], rest[1]


def passed_along(value, by):
    peers = lax.axis_size("section")
    return lax.ppermute(value, "section", [(i, (i + by) % peers) for i in range(peers)])


def route_select(counts, replicas, blocks_dev, capacity):
    blocks = replicas * blocks_dev
    member = jnp.arange(replicas, dtype=jnp.int32)
    ahead = member[:, None] < member[None, :]
    row_start = jnp.sum(jnp.where(ahead[None], counts[:, :, None], 0), axis=1)
    column_start = jnp.sum(jnp.where(ahead[:, :, None], counts[:, None, :], 0), axis=0)
    row_total = row_start + counts
    block_ids = jnp.arange(blocks_dev, dtype=jnp.int32)
    inside = (block_ids[None, :, None] >= row_start[:, None, :]) & (
        block_ids[None, :, None] < row_total[:, None, :]
    )
    member_ids = jnp.arange(replicas, dtype=jnp.int32)
    slot = member_ids[None, None, :] * capacity + (
        column_start[:, None, :] + block_ids[None, :, None] - row_start[:, None, :]
    )
    target = jnp.sum(jnp.where(inside, slot, 0), axis=2).reshape(blocks)
    return target


def one_hot(row_ids, count):
    return (row_ids[:, None] == jnp.arange(count, dtype=jnp.int32)[None, :]).astype(BF16)


def mm(a, b):
    return jnp.dot(a, b, preferred_element_type=F32)


def mm_t(a, b):
    return lax.dot_general(a, b, (((1,), (1,)), ((), ())), preferred_element_type=F32)


def normalize(layer_rows, gain_row):
    values = layer_rows.astype(F32)
    row_scale = lax.rsqrt(jnp.mean(values * values, axis=1, keepdims=True) + epsilon)
    return values, row_scale, (values * row_scale * gain_row[None, :]).astype(BF16)


def low_rank(coefs, factors):
    high = coefs.astype(BF16)
    low = (coefs - high.astype(F32)).astype(BF16)
    return mm(jnp.concatenate((high, low), 1), jnp.concatenate((factors, factors), 0))


def per_device(layer_in, next_in, returned, norm_gain, gate_weight, up_weight, down_weight, wiring):
    replicas = lax.axis_size("rep")
    position = lax.axis_index("rep")
    partner_offset = lax.axis_size("section") // 2
    rows = layer_in.shape[1]
    features = layer_in.shape[2]
    blocks_dev = rows // BLK
    slot_rows = returned.shape[1]
    capacity = slot_rows // BLK
    tokens = rows * replicas
    gain = norm_gain[0]
    gate, up, down = gate_weight[0], up_weight[0], down_weight[0]
    factor = step_rate / tokens

    values, row_scale, normed_own = normalize(layer_in[0], gain)
    next_values, _, next_own = normalize(next_in[0], gain)
    next_mate = passed_along(next_own, partner_offset)
    later = passed_along(returned[0], -1)
    target = route_select(wiring[0], replicas, blocks_dev, capacity)
    width = features // QUARTERS
    mate_shard = next_mate.reshape(rows, QUARTERS, width).transpose(1, 0, 2)
    shards, mate_shards = gather_shards(
        jnp.concatenate((normed_own, next_own, later), 0),
        mate_shard.reshape(QUARTERS * rows, width),
    )
    tall = shards.shape[1]
    shards = shards.reshape(replicas * tall, features)
    mate_shards = mate_shards.reshape(replicas * QUARTERS * rows, width)
    token = jnp.arange(tokens, dtype=jnp.int32)
    member, inner = token // rows, token % rows
    target_rows = (target[:, None] * BLK + jnp.arange(BLK, dtype=jnp.int32)[None, :]).reshape(-1)
    slot_source = target_rows // slot_rows * tall + 2 * rows + target_rows % slot_rows
    picked = mm(
        one_hot(
            jnp.concatenate((slot_source, member * tall + inner, member * tall + rows + inner)),
            replicas * tall,
        ),
        shards,
    ).astype(BF16)
    mate_rows = member * QUARTERS * rows + inner
    nexts_mate = jnp.concatenate(
        [
            mm(one_hot(mate_rows + q * rows, replicas * QUARTERS * rows), mate_shards)
            for q in range(QUARTERS)
        ],
        1,
    ).astype(BF16)
    cotangent = picked[:tokens]
    normed = picked[tokens : 2 * tokens]
    lhs = jnp.concatenate((picked[tokens:], nexts_mate), 0)
    nexts = lhs[tokens:]

    gate_all = mm(lhs, gate)
    up_all = mm(lhs, up)
    gate_act, up_act = gate_all[:tokens], up_all[:tokens]
    sigmoid = jax.nn.sigmoid(gate_act)
    silu = gate_act * sigmoid
    hidden = (silu * up_act).astype(BF16)
    dhidden = mm_t(cotangent, down)
    d_gate = (dhidden * up_act * sigmoid * (1.0 + gate_act * (1.0 - sigmoid))).astype(BF16)
    d_up = (dhidden * silu).astype(BF16)

    coefs = factor * mm_t(nexts, normed)
    next_gate = 0.5 * (gate_all[tokens:] - low_rank(coefs, d_gate))
    next_up = 0.5 * (up_all[tokens:] - low_rank(coefs, d_up))
    to_mate = jnp.stack((next_gate[tokens:], next_up[tokens:])).astype(BF16)
    from_mate = passed_along(to_mate, partner_offset).astype(F32)

    dterm = (mm_t(d_gate, gate) + mm_t(d_up, up)).astype(BF16)
    term = mm(hidden, down)
    own = lax.dynamic_slice_in_dim(term, position * rows, rows, 0) + values
    term = lax.dynamic_update_slice_in_dim(term, own, position * rows, 0).astype(BF16)
    slot_ids = jnp.arange(replicas * slot_rows, dtype=jnp.int32)
    select = (slot_ids[:, None] == target_rows[None, :]).astype(BF16)
    slot_term = mm(select, term).astype(BF16).reshape(replicas, slot_rows, features)
    slot_terms = [slot_term[:, at : at + rows] for at in range(0, slot_rows, rows)]

    gate_next = next_gate[:tokens] + from_mate[0]
    up_next = next_up[:tokens] + from_mate[1]
    hidden_own = (jax.nn.silu(gate_next) * up_next).astype(BF16)
    hidden_mate = passed_along(hidden_own, partner_offset)
    hidden_both = jnp.concatenate((hidden_own, hidden_mate), 0)
    down_coefs = factor * mm_t(hidden_both, hidden)
    term_next = (0.5 * (mm(hidden_both, down) - low_rank(down_coefs, cotangent))).astype(BF16)
    term_next = term_next.reshape(2, replicas, rows, features)
    mate_sum, slots, dnormed, own_sum = sum_terms(
        term_next[1], slot_terms, dterm.reshape(replicas, rows, features), term_next[0]
    )
    next_out = (own_sum + mate_sum + next_values).astype(BF16)
    forwarded = slots.reshape(slot_rows, features)
    scaled = gain[None, :] * dnormed
    cotangent_own = lax.dynamic_slice_in_dim(cotangent, position * rows, rows, 0)
    input_grad = (
        cotangent_own.astype(F32)
        + row_scale * scaled
        - values * row_scale**3 * jnp.mean(values * scaled, axis=1, keepdims=True)
    ).astype(BF16)
    return (forwarded[None], input_grad[None], next_out[None])


def solution(mesh):
    in_specs = (
        P("section", "rep", None),
        P("section", "rep", None),
        P("section", "rep", None),
        P("section", None),
        P("section", None, "rep"),
        P("section", None, "rep"),
        P("section", "rep", None),
        P("section", None, None),
    )
    out_specs = (P("section", "rep", None), P("section", "rep", None), P("section", "rep", None))
    return jax.shard_map(
        per_device, mesh=mesh, in_specs=in_specs, out_specs=out_specs, check_vma=False
    )
```

```python
import functools

import jax
import jax.numpy as jnp
from jax import lax
from jax.experimental import pallas as pl
from jax.experimental.pallas import tpu as pltpu
from jax.sharding import PartitionSpec as P

BLK = 2
epsilon = 1e-05
step_rate = 0.5
F32 = jnp.float32
BF16 = jnp.bfloat16


QUARTERS = 4
CORES = 2
DEPTH_Z = 4


def place(ny):
    me = lax.axis_index("rep")

    def index(z, y, core):
        return (z * ny + y) * CORES + core

    return me // (CORES * ny), (me // CORES) % ny, me % CORES, index


def greet(ny, z, y, core, index, across=()):
    barrier = pltpu.get_barrier_semaphore()
    peers = [{"rep": index((z + d) % DEPTH_Z, y, core)} for d in range(1, DEPTH_Z)]
    peers += [{"rep": index(z, (y + d) % ny, core)} for d in range(1, ny)]
    peers += [{"rep": index(z, y, 1 - core)}]
    peers += [{"section": section} for section in across]
    for peer in peers:
        pl.semaphore_signal(
            barrier, inc=1, device_id=peer, device_id_type=pl.DeviceIdType.MESH
        )
    pl.semaphore_wait(barrier, len(peers))


def remote(src, dst, send, recv, peer):
    return pltpu.make_async_remote_copy(
        src_ref=src,
        dst_ref=dst,
        send_sem=send,
        recv_sem=recv,
        device_id=peer if isinstance(peer, dict) else {"rep": peer},
        device_id_type=pl.DeviceIdType.MESH,
    )


def routing_matrices(counts, rows, blocks_dev, capacity, groups):
    replicas = counts.shape[0]
    tokens = replicas * rows

    def iota(shape, axis):
        return lax.broadcasted_iota(jnp.int32, shape, axis)

    square = (replicas, replicas)
    counts = counts.astype(F32)
    ahead = (iota(square, 0) < iota(square, 1)).astype(F32)
    behind = (iota(square, 1) < iota(square, 0)).astype(F32)
    row_start = mm(counts, ahead)
    column_start = mm(behind, counts)
    receiver = iota(square, 1).astype(F32)
    spread = jnp.ones((replicas, tokens), F32)
    target = (iota((tokens, tokens), 0) % BLK).astype(F32)
    owner = iota((tokens, replicas), 0) // rows == iota((tokens, replicas), 1)
    block = iota((tokens, replicas), 0) % rows // BLK
    for b in range(blocks_dev):
        inside = (row_start <= b) & (row_start + counts > b)
        slot = jnp.where(inside, receiver * capacity + column_start + b - row_start, 0.0)
        rows_of = (owner & (block == b)).astype(F32)
        target = target + BLK * mm(rows_of, mm(slot, spread))
    lane = iota((tokens, tokens), 1)
    place_of = lane // rows * (rows * groups) + lane % rows
    return [(target == (place_of + g * rows).astype(F32)).astype(F32) for g in range(groups)]


def gather_kernel(
    ny, rows, blocks_dev, head_ref, back_ref, wiring_ref, head, back, mates, select, send, send_x, recv
):
    z, y, core, index = place(ny)
    sections = lax.axis_size("section")
    section = lax.axis_index("section")
    mate = (section + sections // 2) % sections
    following = (section + 1) % sections
    before = (section + sections - 1) % sections
    greet(ny, z, y, core, index, (mate, following, before))
    me = index(z, y, core)
    sibling = index(z, y, 1 - core)
    outs = (head, back, mates)
    width = mates.shape[2]

    def hop(kind, way, shard, peer):
        out = outs[kind].at[shard]
        return remote(out, out, send.at[kind, way, shard], recv.at[kind, shard], peer)

    def over_x(shard):
        return remote(
            head.at[shard, :, pl.ds(width, width)],
            mates.at[shard],
            send_x.at[shard],
            recv.at[2, shard],
            {"section": mate},
        )

    def arrive(kind, shard):
        hop(kind, 0, shard, sibling).wait_recv()

    back_copy = remote(
        back_ref, back.at[me], send_x.at[send_x.shape[0] - 1], recv.at[1, me], {"section": before}
    )
    head[me] = head_ref[...]
    back_copy.start()

    def arrivals(d):
        for step in (1, -1) if d else (0,):
            yield step, z - step * d, (z - step * d >= 0) & (z - step * d < DEPTH_Z)

    def onward(kind, d, step, zz, act):
        shard = index(zz, y, core)
        for way, to in enumerate((1, -1)):
            if step in (0, to):

                @pl.when((z + to >= 0) & (z + to < DEPTH_Z))
                def _():
                    act(hop(kind, way, shard, index(z + to, y, core)))

        for dy in range(1, ny):
            act(hop(kind, 2 + dy, shard, index(z, (y + dy) % ny, core)))
        act(hop(kind, 2, shard, sibling))
        if kind == 0:
            act(over_x(shard))

    def along_z(d):
        for kind in range(2):
            for step, zz, there in arrivals(d):

                @pl.when(there)
                def _():
                    if d or kind:
                        arrive(kind, index(zz, y, core))
                    onward(kind, d, step, zz, lambda copy: copy.start())

    def from_y(d):
        for kind in range(2):
            for step, zz, there in arrivals(d):

                @pl.when(there)
                def _():
                    for dy in range(1, ny):
                        shard = index(zz, (y + dy) % ny, core)
                        arrive(kind, shard)
                        hop(kind, 2, shard, sibling).start()
                        if kind == 0:
                            over_x(shard).start()

    along_z(0)
    matrices = routing_matrices(
        wiring_ref[...], rows, blocks_dev, select.shape[0] * rows // BLK, select.shape[0]
    )
    for g, matrix in enumerate(matrices):
        select[g] = matrix.astype(BF16)
    for d in range(1, DEPTH_Z):
        along_z(d)
        from_y(d - 1)
    from_y(DEPTH_Z - 1)
    every = [(dz, dy) for dy in range(ny) for dz in range(DEPTH_Z)]
    for dz, dy in every:
        shard = index((z + dz) % DEPTH_Z, (y + dy) % ny, core)
        arrive(2, shard)
        hop(2, 2, shard, sibling).start()
    for kind in range(3):
        for dz, dy in every:
            arrive(kind, index((z + dz) % DEPTH_Z, (y + dy) % ny, 1 - core))
    back_copy.wait_send()
    for kind in range(2):
        for d in range(DEPTH_Z):
            for step, zz, there in arrivals(d):

                @pl.when(there)
                def _():
                    onward(kind, d, step, zz, lambda copy: copy.wait_send())
                    for dy in range(1, ny):
                        shard = index(zz, (y + dy) % ny, core)
                        hop(kind, 2, shard, sibling).wait_send()
                        if kind == 0:
                            over_x(shard).wait_send()

    for dz, dy in every:
        hop(2, 2, index((z + dz) % DEPTH_Z, (y + dy) % ny, core), sibling).wait_send()


def gather_shards(head, back, wiring, rows, blocks_dev):
    replicas = lax.axis_size("rep")
    ny = replicas // (CORES * DEPTH_Z)
    tokens = replicas * rows
    tall, wide = head.shape
    groups = back.shape[1] // (wide // 2)
    vmem = pl.BlockSpec(memory_space=pltpu.VMEM)
    return pl.pallas_call(
        functools.partial(gather_kernel, ny, rows, blocks_dev),
        out_shape=[
            jax.ShapeDtypeStruct((replicas,) + head.shape, BF16),
            jax.ShapeDtypeStruct((replicas,) + back.shape, BF16),
            jax.ShapeDtypeStruct((replicas, tall, wide // 2), BF16),
            jax.ShapeDtypeStruct((groups, tokens, tokens), BF16),
        ],
        in_specs=[vmem] * 3,
        out_specs=[vmem] * 4,
        scratch_shapes=[
            pltpu.SemaphoreType.DMA((3, 2 + ny, replicas)),
            pltpu.SemaphoreType.DMA((replicas + 1,)),
            pltpu.SemaphoreType.DMA((3, replicas)),
        ],
        compiler_params=pltpu.CompilerParams(
            collective_id=0, has_side_effects=True, vmem_limit_bytes=32 * 2**20
        ),
    )(head, back, wiring)


def sum_kernel(ny, routed, *refs):
    kinds = routed + 3
    terms = refs[:kinds]
    slots_out, rest_out = refs[kinds : kinds + 2]
    from_core, part, from_y, summed, from_z, to_x, from_x, slot_sum = refs[kinds + 2 : kinds + 10]
    send, recv_core, recv_y, recv_z, recv_x, recv_slot = refs[kinds + 10 :]
    z, y, core, index = place(ny)
    sections = lax.axis_size("section")
    section = lax.axis_index("section")
    mate = (section + sections // 2) % sections
    following = (section + 1) % sections
    before = (section + sections - 1) % sections
    greet(ny, z, y, core, index, (mate, following, before))
    sibling = index(z, y, 1 - core)
    started = []

    def push(src, dst, recv, peer):
        copy = remote(src, dst, send.at[len(started)], recv, peer)
        copy.start()
        started.append(copy)
        return copy

    y_order = list(range(1, ny)) + [0]
    z_order = list(range(2, DEPTH_Z - 1)) + [1, DEPTH_Z - 1, 0]
    core_copies, y_copies, z_copies, totals = {}, {}, {}, {}
    for k in range(kinds):
        for dy in y_order:
            yy = (y + dy) % ny
            core_copies[k, dy] = push(
                terms[k].at[1 - core, yy], from_core.at[k, yy], recv_core.at[k, dy], sibling
            )

    x_copies = {}
    for dy in y_order:
        yy = (y + dy) % ny
        core_copies[0, dy].wait_recv()
        to_x[yy] = (terms[0][core, yy].astype(F32) + from_core[0, yy].astype(F32)).astype(BF16)
        x_copies[dy] = push(to_x.at[yy], from_x.at[yy], recv_x.at[dy], {"section": mate})

    def pair_sum(k, yy, zz=slice(None)):
        total = terms[k][core, yy, zz].astype(F32) + from_core[k, yy, zz].astype(F32)
        if k == kinds - 1:
            total = total + from_x[yy, zz].astype(F32)
        return total

    def to_y(k):
        for dy in y_order[:-1]:
            yy = (y + dy) % ny
            core_copies[k, dy].wait_recv()
            if k == kinds - 1:
                x_copies[dy].wait_recv()
            part[k, dy - 1] = pair_sum(k, yy).astype(BF16)
            y_copies[k, dy] = push(
                part.at[k, dy - 1],
                from_y.at[k, dy - 1],
                recv_y.at[k, dy - 1],
                index(z, yy, core),
            )

    def to_z(k):
        core_copies[k, 0].wait_recv()
        if k == kinds - 1:
            x_copies[0].wait_recv()
        for dy in y_order[:-1]:
            y_copies[k, dy].wait_recv()
        for dz in z_order:
            zz = (z + dz) % DEPTH_Z
            total = pair_sum(k, y, zz)
            for dy in range(1, ny):
                total = total + from_y[k, dy - 1, zz].astype(F32)
            if dz:
                summed[k, dz - 1] = total.astype(BF16)
                z_copies[k, dz] = push(
                    summed.at[k, dz - 1],
                    from_z.at[k, dz - 1],
                    recv_z.at[k, dz - 1],
                    index(zz, y, core),
                )
        totals[k] = total

    slot_copies = []

    def finish(k):
        total = totals[k]
        for dz in z_order[:-1]:
            z_copies[k, dz].wait_recv()
            total = total + from_z[k, dz - 1].astype(F32)
        if k <= routed:
            slot_sum[k - 1] = total.astype(BF16)
            slot_copies.append(
                push(
                    slot_sum.at[k - 1],
                    slots_out.at[k - 1],
                    recv_slot.at[k - 1],
                    {"section": following},
                )
            )
        else:
            rest_out[k - routed - 1] = total

    for k in range(1, kinds + 2):
        if k < kinds:
            to_y(k)
        if 2 <= k <= kinds:
            to_z(k - 1)
        if k >= 3:
            finish(k - 2)
    for copy in slot_copies:
        copy.wait_recv()
    for copy in started:
        copy.wait_send()


def lay_terms(terms):
    replicas, rows, features = terms.shape
    ny = replicas // (CORES * DEPTH_Z)
    width = features // QUARTERS
    laid = terms.reshape(DEPTH_Z, ny, CORES, rows, QUARTERS, width)
    return laid.transpose(2, 1, 0, 4, 3, 5).reshape(CORES, ny, DEPTH_Z, rows * QUARTERS, width)


def lay_back(value, rows):
    tall, width = value.shape[-2:]
    value = value.reshape(-1, QUARTERS, rows, width).transpose(0, 2, 1, 3)
    return value.reshape(-1, rows, QUARTERS * width)


def sum_terms(mate_terms, slot_terms, d_terms, own_terms):
    laid = [lay_terms(v) for v in (mate_terms, *slot_terms, d_terms, own_terms)]
    _, ny, _, tall, width = laid[0].shape
    routed = len(slot_terms)
    kinds = len(laid)
    rows = mate_terms.shape[1]
    copies = kinds * (ny + ny - 1 + DEPTH_Z - 1) + ny + routed
    vmem = pl.BlockSpec(memory_space=pltpu.VMEM)
    slots, rest = pl.pallas_call(
        functools.partial(sum_kernel, ny, routed),
        out_shape=[
            jax.ShapeDtypeStruct((routed, tall, width), BF16),
            jax.ShapeDtypeStruct((2, tall, width), F32),
        ],
        in_specs=[vmem] * kinds,
        out_specs=[vmem] * 2,
        scratch_shapes=[
            pltpu.VMEM((kinds, ny, DEPTH_Z, tall, width), BF16),
            pltpu.VMEM((kinds, ny - 1, DEPTH_Z, tall, width), BF16),
            pltpu.VMEM((kinds, ny - 1, DEPTH_Z, tall, width), BF16),
            pltpu.VMEM((kinds, DEPTH_Z - 1, tall, width), BF16),
            pltpu.VMEM((kinds, DEPTH_Z - 1, tall, width), BF16),
            pltpu.VMEM((ny, DEPTH_Z, tall, width), BF16),
            pltpu.VMEM((ny, DEPTH_Z, tall, width), BF16),
            pltpu.VMEM((routed, tall, width), BF16),
            pltpu.SemaphoreType.DMA((copies,)),
            pltpu.SemaphoreType.DMA((kinds, ny)),
            pltpu.SemaphoreType.DMA((kinds, ny - 1)),
            pltpu.SemaphoreType.DMA((kinds, DEPTH_Z - 1)),
            pltpu.SemaphoreType.DMA((ny,)),
            pltpu.SemaphoreType.DMA((routed,)),
        ],
        compiler_params=pltpu.CompilerParams(
            collective_id=1, has_side_effects=True, vmem_limit_bytes=40 * 2**20
        ),
    )(*laid)
    rest = lay_back(rest, rows)
    return lay_back(slots, rows), rest[0], rest[1]


def passed_along(value, by):
    peers = lax.axis_size("section")
    return lax.ppermute(value, "section", [(i, (i + by) % peers) for i in range(peers)])


def one_hot(row_ids, count):
    return (row_ids[:, None] == jnp.arange(count, dtype=jnp.int32)[None, :]).astype(BF16)


def mm(a, b):
    return jnp.dot(a, b, preferred_element_type=F32)


def mm_t(a, b):
    return lax.dot_general(a, b, (((1,), (1,)), ((), ())), preferred_element_type=F32)


def normalize(layer_rows, gain_row):
    values = layer_rows.astype(F32)
    row_scale = lax.rsqrt(jnp.mean(values * values, axis=1, keepdims=True) + epsilon)
    return values, row_scale, (values * row_scale * gain_row[None, :]).astype(BF16)


def low_rank(coefs, factors):
    high = coefs.astype(BF16)
    low = (coefs - high.astype(F32)).astype(BF16)
    return mm(jnp.concatenate((high, low), 1), jnp.concatenate((factors, factors), 0))


def per_device(layer_in, next_in, returned, norm_gain, gate_weight, up_weight, down_weight, wiring):
    replicas = lax.axis_size("rep")
    position = lax.axis_index("rep")
    partner_offset = lax.axis_size("section") // 2
    rows = layer_in.shape[1]
    features = layer_in.shape[2]
    blocks_dev = rows // BLK
    slot_rows = returned.shape[1]
    tokens = rows * replicas
    gain = norm_gain[0]
    gate, up, down = gate_weight[0], up_weight[0], down_weight[0]
    factor = step_rate / tokens

    values, row_scale, normed_own = normalize(layer_in[0], gain)
    next_values, _, next_own = normalize(next_in[0], gain)
    width = features // QUARTERS

    def quartered(value):
        groups = value.reshape(-1, rows, QUARTERS, width).transpose(2, 1, 0, 3)
        return groups.reshape(QUARTERS * rows, -1)

    head, back, mates, select = gather_shards(
        quartered(jnp.concatenate((normed_own, next_own), 0)),
        quartered(returned[0]),
        wiring[0],
        rows,
        blocks_dev,
    )
    token = jnp.arange(tokens, dtype=jnp.int32)
    quarter_rows = token // rows * QUARTERS * rows + token % rows

    def compact(value):
        flat = value.reshape(replicas * QUARTERS * rows, -1)
        parts = [
            mm(one_hot(quarter_rows + q * rows, flat.shape[0]), flat).astype(BF16)
            for q in range(QUARTERS)
        ]
        return [
            jnp.concatenate([part[:, at : at + width] for part in parts], 1)
            for at in range(0, flat.shape[1], width)
        ]

    normed, nexts_own = compact(head)
    (nexts_mate,) = compact(mates)
    slots = jnp.concatenate(compact(back), 0)
    groups = select.shape[0]
    cotangent = mm(select.transpose(1, 0, 2).reshape(tokens, groups * tokens), slots).astype(BF16)
    lhs = jnp.concatenate((normed, nexts_own, nexts_mate), 0)
    nexts = lhs[tokens:]

    gate_all = mm(lhs, gate)
    up_all = mm(lhs, up)
    gate_act, up_act = gate_all[:tokens], up_all[:tokens]
    sigmoid = jax.nn.sigmoid(gate_act)
    silu = gate_act * sigmoid
    hidden = (silu * up_act).astype(BF16)
    dhidden = mm_t(cotangent, down)
    d_gate = (dhidden * up_act * sigmoid * (1.0 + gate_act * (1.0 - sigmoid))).astype(BF16)
    d_up = (dhidden * silu).astype(BF16)

    coefs = factor * mm_t(nexts, normed)
    next_gate = 0.5 * (gate_all[tokens:] - low_rank(coefs, d_gate))
    next_up = 0.5 * (up_all[tokens:] - low_rank(coefs, d_up))
    to_mate = jnp.stack((next_gate[tokens:], next_up[tokens:])).astype(BF16)
    from_mate = passed_along(to_mate, partner_offset).astype(F32)

    dterm = (mm_t(d_gate, gate) + mm_t(d_up, up)).astype(BF16)
    term = mm(hidden, down)
    own = lax.dynamic_slice_in_dim(term, position * rows, rows, 0) + values
    term = lax.dynamic_update_slice_in_dim(term, own, position * rows, 0).astype(BF16)
    slot_terms = [
        lax.dot_general(
            select[g], term, (((0,), (0,)), ((), ())), preferred_element_type=F32
        )
        .astype(BF16)
        .reshape(replicas, rows, features)
        for g in range(groups)
    ]

    gate_next = next_gate[:tokens] + from_mate[0]
    up_next = next_up[:tokens] + from_mate[1]
    hidden_own = (jax.nn.silu(gate_next) * up_next).astype(BF16)
    hidden_mate = passed_along(hidden_own, partner_offset)
    hidden_both = jnp.concatenate((hidden_own, hidden_mate), 0)
    down_coefs = factor * mm_t(hidden_both, hidden)
    term_next = (0.5 * (mm(hidden_both, down) - low_rank(down_coefs, cotangent))).astype(BF16)
    term_next = term_next.reshape(2, replicas, rows, features)
    slots, dnormed, own_sum = sum_terms(
        term_next[1], slot_terms, dterm.reshape(replicas, rows, features), term_next[0]
    )
    next_out = (own_sum + next_values).astype(BF16)
    forwarded = slots.reshape(slot_rows, features)
    scaled = gain[None, :] * dnormed
    cotangent_own = lax.dynamic_slice_in_dim(cotangent, position * rows, rows, 0)
    input_grad = (
        cotangent_own.astype(F32)
        + row_scale * scaled
        - values * row_scale**3 * jnp.mean(values * scaled, axis=1, keepdims=True)
    ).astype(BF16)
    return (forwarded[None], input_grad[None], next_out[None])


def solution(mesh):
    in_specs = (
        P("section", "rep", None),
        P("section", "rep", None),
        P("section", "rep", None),
        P("section", None),
        P("section", None, "rep"),
        P("section", None, "rep"),
        P("section", "rep", None),
        P("section", None, None),
    )
    out_specs = (P("section", "rep", None), P("section", "rep", None), P("section", "rep", None))
    return jax.shard_map(
        per_device, mesh=mesh, in_specs=in_specs, out_specs=out_specs, check_vma=False
    )
```

```python
import functools

import jax
import jax.numpy as jnp
from jax import lax
from jax.experimental import pallas as pl
from jax.experimental.pallas import tpu as pltpu
from jax.sharding import PartitionSpec as P

BLK = 2
epsilon = 1e-05
step_rate = 0.5
F32 = jnp.float32
BF16 = jnp.bfloat16


QUARTERS = 4
CORES = 2
DEPTH_Z = 4


def place(ny):
    me = lax.axis_index("rep")

    def index(z, y, core):
        return (z * ny + y) * CORES + core

    return me // (CORES * ny), (me // CORES) % ny, me % CORES, index


def greet(ny, z, y, core, index, across=()):
    barrier = pltpu.get_barrier_semaphore()
    peers = [{"rep": index((z + d) % DEPTH_Z, y, core)} for d in range(1, DEPTH_Z)]
    peers += [{"rep": index(z, (y + d) % ny, core)} for d in range(1, ny)]
    peers += [{"rep": index(z, y, 1 - core)}]
    peers += [{"section": section} for section in across]
    for peer in peers:
        pl.semaphore_signal(
            barrier, inc=1, device_id=peer, device_id_type=pl.DeviceIdType.MESH
        )
    pl.semaphore_wait(barrier, len(peers))


def remote(src, dst, send, recv, peer):
    return pltpu.make_async_remote_copy(
        src_ref=src,
        dst_ref=dst,
        send_sem=send,
        recv_sem=recv,
        device_id=peer if isinstance(peer, dict) else {"rep": peer},
        device_id_type=pl.DeviceIdType.MESH,
    )


def routing_matrices(counts, rows, blocks_dev, capacity, groups):
    replicas = counts.shape[0]
    tokens = replicas * rows

    def iota(shape, axis):
        return lax.broadcasted_iota(jnp.int32, shape, axis)

    square = (replicas, replicas)
    counts = counts.astype(F32)
    ahead = (iota(square, 0) < iota(square, 1)).astype(F32)
    behind = (iota(square, 1) < iota(square, 0)).astype(F32)
    row_start = mm(counts, ahead)
    column_start = mm(behind, counts)
    receiver = iota(square, 1).astype(F32)
    raw = tokens * QUARTERS
    spread = jnp.ones((replicas, raw), F32)
    spread_down = jnp.ones((groups * tokens, replicas), F32)
    target = (iota((tokens, raw), 0) % BLK).astype(F32)
    target_down = (iota((groups * tokens, tokens), 1) % BLK).astype(F32)
    owner = iota((tokens, replicas), 0) // rows == iota((tokens, replicas), 1)
    block = iota((tokens, replicas), 0) % rows // BLK
    for b in range(blocks_dev):
        inside = (row_start <= b) & (row_start + counts > b)
        slot = jnp.where(inside, receiver * capacity + column_start + b - row_start, 0.0)
        rows_of = (owner & (block == b)).astype(F32)
        target = target + BLK * mm(rows_of, mm(slot, spread))
        target_down = target_down + BLK * mm_t(mm_t(spread_down, slot), rows_of)
    lane = iota((tokens, raw), 1)
    quarter = lane % (QUARTERS * rows) // rows
    slot_row = lane // (QUARTERS * rows) * (rows * groups) + lane % rows
    picks = [
        [
            ((target == (slot_row + g * rows).astype(F32)) & (quarter == q)).astype(F32)
            for g in range(groups)
        ]
        for q in range(QUARTERS)
    ]
    line = iota((groups * tokens, tokens), 0)
    inner = line % tokens
    sent = inner // rows * (rows * groups) + line // tokens * rows + inner % rows
    own = iota((tokens, raw), 0)
    own = own // rows * (QUARTERS * rows) + own % rows
    compact = [(lane == own + q * rows).astype(F32) for q in range(QUARTERS)]
    return picks, compact, (target_down == sent.astype(F32)).astype(F32)


def gather_kernel(
    ny, rows, blocks_dev, head_ref, back_ref, wiring_ref, lhs, cotangent, select,
    head, back, mates, send, send_x, recv
):
    z, y, core, index = place(ny)
    sections = lax.axis_size("section")
    section = lax.axis_index("section")
    mate = (section + sections // 2) % sections
    following = (section + 1) % sections
    before = (section + sections - 1) % sections
    greet(ny, z, y, core, index, (mate, following, before))
    me = index(z, y, core)
    sibling = index(z, y, 1 - core)
    outs = (head, back, mates)
    width = mates.shape[2]

    def hop(kind, way, shard, peer):
        out = outs[kind].at[shard]
        return remote(out, out, send.at[kind, way, shard], recv.at[kind, shard], peer)

    def over_x(shard):
        return remote(
            head.at[shard, :, pl.ds(width, width)],
            mates.at[shard],
            send_x.at[shard],
            recv.at[2, shard],
            {"section": mate},
        )

    def arrive(kind, shard):
        hop(kind, 0, shard, sibling).wait_recv()

    back_copy = remote(
        back_ref, back.at[me], send_x.at[send_x.shape[0] - 1], recv.at[1, me], {"section": before}
    )
    head[me] = head_ref[...]
    back_copy.start()

    def arrivals(d):
        for step in (1, -1) if d else (0,):
            yield step, z - step * d, (z - step * d >= 0) & (z - step * d < DEPTH_Z)

    def onward(kind, d, step, zz, act):
        shard = index(zz, y, core)
        for way, to in enumerate((1, -1)):
            if step in (0, to):

                @pl.when((z + to >= 0) & (z + to < DEPTH_Z))
                def _():
                    act(hop(kind, way, shard, index(z + to, y, core)))

        for dy in range(1, ny):
            act(hop(kind, 2 + dy, shard, index(z, (y + dy) % ny, core)))
        act(hop(kind, 2, shard, sibling))
        if kind == 0:
            act(over_x(shard))

    def along_z(d):
        for kind in range(2):
            for step, zz, there in arrivals(d):

                @pl.when(there)
                def _():
                    if d or kind:
                        arrive(kind, index(zz, y, core))
                    onward(kind, d, step, zz, lambda copy: copy.start())

    def from_y(d):
        for kind in range(2):
            for step, zz, there in arrivals(d):

                @pl.when(there)
                def _():
                    for dy in range(1, ny):
                        shard = index(zz, (y + dy) % ny, core)
                        arrive(kind, shard)
                        hop(kind, 2, shard, sibling).start()
                        if kind == 0:
                            over_x(shard).start()

    along_z(0)
    tokens = cotangent.shape[0]
    groups = back.shape[2] // width
    picks, compact, sent = routing_matrices(
        wiring_ref[...], rows, blocks_dev, groups * rows // BLK, groups
    )
    select[...] = sent.astype(BF16)
    for d in range(1, DEPTH_Z):
        along_z(d)
        from_y(d - 1)
    from_y(DEPTH_Z - 1)
    every = [(dz, dy) for dy in range(ny) for dz in range(DEPTH_Z)]
    for dz, dy in every:
        shard = index((z + dz) % DEPTH_Z, (y + dy) % ny, core)
        arrive(2, shard)
        hop(2, 2, shard, sibling).start()
    for kind in range(3):
        for dz, dy in every:
            arrive(kind, index((z + dz) % DEPTH_Z, (y + dy) % ny, 1 - core))
    flat = [out[...].reshape(tokens * QUARTERS, out.shape[2]) for out in outs]
    for q in range(QUARTERS):
        columns = slice(q * width, (q + 1) * width)
        pick = compact[q].astype(BF16)
        both = mm(pick, flat[0]).astype(BF16)
        lhs[:tokens, columns] = both[:, :width]
        lhs[tokens : 2 * tokens, columns] = both[:, width:]
        lhs[2 * tokens :, columns] = mm(pick, flat[2]).astype(BF16)
        cot = sum(
            mm(picks[q][g].astype(BF16), flat[1][:, g * width : (g + 1) * width])
            for g in range(groups)
        )
        cotangent[:, columns] = cot.astype(BF16)
    back_copy.wait_send()
    for kind in range(2):
        for d in range(DEPTH_Z):
            for step, zz, there in arrivals(d):

                @pl.when(there)
                def _():
                    onward(kind, d, step, zz, lambda copy: copy.wait_send())
                    for dy in range(1, ny):
                        shard = index(zz, (y + dy) % ny, core)
                        hop(kind, 2, shard, sibling).wait_send()
                        if kind == 0:
                            over_x(shard).wait_send()

    for dz, dy in every:
        hop(2, 2, index((z + dz) % DEPTH_Z, (y + dy) % ny, core), sibling).wait_send()


def gather_shards(head, back, wiring, rows, blocks_dev):
    replicas = lax.axis_size("rep")
    ny = replicas // (CORES * DEPTH_Z)
    tokens = replicas * rows
    tall, wide = head.shape
    groups = back.shape[1] // (wide // 2)
    vmem = pl.BlockSpec(memory_space=pltpu.VMEM)
    return pl.pallas_call(
        functools.partial(gather_kernel, ny, rows, blocks_dev),
        out_shape=[
            jax.ShapeDtypeStruct((3 * tokens, QUARTERS * wide // 2), BF16),
            jax.ShapeDtypeStruct((tokens, QUARTERS * wide // 2), BF16),
            jax.ShapeDtypeStruct((groups * tokens, tokens), BF16),
        ],
        in_specs=[vmem] * 3,
        out_specs=[vmem] * 3,
        scratch_shapes=[
            pltpu.VMEM((replicas,) + head.shape, BF16),
            pltpu.VMEM((replicas,) + back.shape, BF16),
            pltpu.VMEM((replicas, tall, wide // 2), BF16),
            pltpu.SemaphoreType.DMA((3, 2 + ny, replicas)),
            pltpu.SemaphoreType.DMA((replicas + 1,)),
            pltpu.SemaphoreType.DMA((3, replicas)),
        ],
        compiler_params=pltpu.CompilerParams(
            collective_id=0, has_side_effects=True, vmem_limit_bytes=20 * 2**20
        ),
    )(head, back, wiring)


def sum_kernel(ny, routed, *refs):
    kinds = routed + 3
    terms = refs[:kinds]
    slots_out, rest_out = refs[kinds : kinds + 2]
    from_core, part, from_y, summed, from_z, to_x, from_x, slot_sum = refs[kinds + 2 : kinds + 10]
    send, recv_core, recv_y, recv_z, recv_x, recv_slot = refs[kinds + 10 :]
    z, y, core, index = place(ny)
    sections = lax.axis_size("section")
    section = lax.axis_index("section")
    mate = (section + sections // 2) % sections
    following = (section + 1) % sections
    before = (section + sections - 1) % sections
    greet(ny, z, y, core, index, (mate, following, before))
    sibling = index(z, y, 1 - core)
    started = []

    def push(src, dst, recv, peer):
        copy = remote(src, dst, send.at[len(started)], recv, peer)
        copy.start()
        started.append(copy)
        return copy

    y_order = list(range(1, ny)) + [0]
    z_order = list(range(2, DEPTH_Z - 1)) + [1, DEPTH_Z - 1, 0]
    core_copies, y_copies, z_copies, totals = {}, {}, {}, {}
    for k in range(kinds):
        for dy in y_order:
            yy = (y + dy) % ny
            core_copies[k, dy] = push(
                terms[k].at[1 - core, yy], from_core.at[k, yy], recv_core.at[k, dy], sibling
            )

    x_copies = {}
    for dy in y_order:
        yy = (y + dy) % ny
        core_copies[0, dy].wait_recv()
        to_x[yy] = (terms[0][core, yy].astype(F32) + from_core[0, yy].astype(F32)).astype(BF16)
        x_copies[dy] = push(to_x.at[yy], from_x.at[yy], recv_x.at[dy], {"section": mate})

    def pair_sum(k, yy, zz=slice(None)):
        total = terms[k][core, yy, zz].astype(F32) + from_core[k, yy, zz].astype(F32)
        if k == kinds - 1:
            total = total + from_x[yy, zz].astype(F32)
        return total

    def to_y(k):
        for dy in y_order[:-1]:
            yy = (y + dy) % ny
            core_copies[k, dy].wait_recv()
            if k == kinds - 1:
                x_copies[dy].wait_recv()
            part[k, dy - 1] = pair_sum(k, yy).astype(BF16)
            y_copies[k, dy] = push(
                part.at[k, dy - 1],
                from_y.at[k, dy - 1],
                recv_y.at[k, dy - 1],
                index(z, yy, core),
            )

    def to_z(k):
        core_copies[k, 0].wait_recv()
        if k == kinds - 1:
            x_copies[0].wait_recv()
        for dy in y_order[:-1]:
            y_copies[k, dy].wait_recv()
        for dz in z_order:
            zz = (z + dz) % DEPTH_Z
            total = pair_sum(k, y, zz)
            for dy in range(1, ny):
                total = total + from_y[k, dy - 1, zz].astype(F32)
            if dz:
                summed[k, dz - 1] = total.astype(BF16)
                z_copies[k, dz] = push(
                    summed.at[k, dz - 1],
                    from_z.at[k, dz - 1],
                    recv_z.at[k, dz - 1],
                    index(zz, y, core),
                )
        totals[k] = total

    slot_copies = []

    def finish(k):
        total = totals[k]
        for dz in z_order[:-1]:
            z_copies[k, dz].wait_recv()
            total = total + from_z[k, dz - 1].astype(F32)
        if k <= routed:
            slot_sum[k - 1] = total.astype(BF16)
            slot_copies.append(
                push(
                    slot_sum.at[k - 1],
                    slots_out.at[k - 1],
                    recv_slot.at[k - 1],
                    {"section": following},
                )
            )
        else:
            rest_out[k - routed - 1] = total

    for k in range(1, kinds + 2):
        if k < kinds:
            to_y(k)
        if 2 <= k <= kinds:
            to_z(k - 1)
        if k >= 3:
            finish(k - 2)
    for copy in slot_copies:
        copy.wait_recv()
    for copy in started:
        copy.wait_send()


def lay_terms(terms):
    replicas, rows, features = terms.shape
    ny = replicas // (CORES * DEPTH_Z)
    width = features // QUARTERS
    laid = terms.reshape(DEPTH_Z, ny, CORES, rows, QUARTERS, width)
    return laid.transpose(2, 1, 0, 4, 3, 5).reshape(CORES, ny, DEPTH_Z, rows * QUARTERS, width)


def lay_back(value, rows):
    tall, width = value.shape[-2:]
    value = value.reshape(-1, QUARTERS, rows, width).transpose(0, 2, 1, 3)
    return value.reshape(-1, rows, QUARTERS * width)


def sum_terms(mate_terms, slot_terms, d_terms, own_terms):
    laid = [lay_terms(v) for v in (mate_terms, *slot_terms, d_terms, own_terms)]
    _, ny, _, tall, width = laid[0].shape
    routed = len(slot_terms)
    kinds = len(laid)
    rows = mate_terms.shape[1]
    copies = kinds * (ny + ny - 1 + DEPTH_Z - 1) + ny + routed
    vmem = pl.BlockSpec(memory_space=pltpu.VMEM)
    slots, rest = pl.pallas_call(
        functools.partial(sum_kernel, ny, routed),
        out_shape=[
            jax.ShapeDtypeStruct((routed, tall, width), BF16),
            jax.ShapeDtypeStruct((2, tall, width), F32),
        ],
        in_specs=[vmem] * kinds,
        out_specs=[vmem] * 2,
        scratch_shapes=[
            pltpu.VMEM((kinds, ny, DEPTH_Z, tall, width), BF16),
            pltpu.VMEM((kinds, ny - 1, DEPTH_Z, tall, width), BF16),
            pltpu.VMEM((kinds, ny - 1, DEPTH_Z, tall, width), BF16),
            pltpu.VMEM((kinds, DEPTH_Z - 1, tall, width), BF16),
            pltpu.VMEM((kinds, DEPTH_Z - 1, tall, width), BF16),
            pltpu.VMEM((ny, DEPTH_Z, tall, width), BF16),
            pltpu.VMEM((ny, DEPTH_Z, tall, width), BF16),
            pltpu.VMEM((routed, tall, width), BF16),
            pltpu.SemaphoreType.DMA((copies,)),
            pltpu.SemaphoreType.DMA((kinds, ny)),
            pltpu.SemaphoreType.DMA((kinds, ny - 1)),
            pltpu.SemaphoreType.DMA((kinds, DEPTH_Z - 1)),
            pltpu.SemaphoreType.DMA((ny,)),
            pltpu.SemaphoreType.DMA((routed,)),
        ],
        compiler_params=pltpu.CompilerParams(
            collective_id=1, has_side_effects=True, vmem_limit_bytes=20 * 2**20
        ),
    )(*laid)
    rest = lay_back(rest, rows)
    return lay_back(slots, rows), rest[0], rest[1]


def passed_along(value, by):
    peers = lax.axis_size("section")
    return lax.ppermute(value, "section", [(i, (i + by) % peers) for i in range(peers)])


def mm(a, b):
    return jnp.dot(a, b, preferred_element_type=F32)


def mm_t(a, b):
    return lax.dot_general(a, b, (((1,), (1,)), ((), ())), preferred_element_type=F32)


def normalize(layer_rows, gain_row):
    values = layer_rows.astype(F32)
    row_scale = lax.rsqrt(jnp.mean(values * values, axis=1, keepdims=True) + epsilon)
    return values, row_scale, (values * row_scale * gain_row[None, :]).astype(BF16)


def low_rank(coefs, factors):
    high = coefs.astype(BF16)
    low = (coefs - high.astype(F32)).astype(BF16)
    return mm(jnp.concatenate((high, low), 1), jnp.concatenate((factors, factors), 0))


def per_device(layer_in, next_in, returned, norm_gain, gate_weight, up_weight, down_weight, wiring):
    replicas = lax.axis_size("rep")
    position = lax.axis_index("rep")
    partner_offset = lax.axis_size("section") // 2
    rows = layer_in.shape[1]
    features = layer_in.shape[2]
    blocks_dev = rows // BLK
    slot_rows = returned.shape[1]
    tokens = rows * replicas
    gain = norm_gain[0]
    gate, up, down = gate_weight[0], up_weight[0], down_weight[0]
    factor = step_rate / tokens

    values, row_scale, normed_own = normalize(layer_in[0], gain)
    next_values, _, next_own = normalize(next_in[0], gain)
    width = features // QUARTERS

    def quartered(value):
        groups = value.reshape(-1, rows, QUARTERS, width).transpose(2, 1, 0, 3)
        return groups.reshape(QUARTERS * rows, -1)

    lhs, cotangent, select = gather_shards(
        quartered(jnp.concatenate((normed_own, next_own), 0)),
        quartered(returned[0]),
        wiring[0],
        rows,
        blocks_dev,
    )
    normed = lhs[:tokens]
    nexts = lhs[tokens:]

    gate_all = mm(lhs, gate)
    up_all = mm(lhs, up)
    gate_act, up_act = gate_all[:tokens], up_all[:tokens]
    sigmoid = jax.nn.sigmoid(gate_act)
    silu = gate_act * sigmoid
    hidden = (silu * up_act).astype(BF16)
    dhidden = mm_t(cotangent, down)
    d_gate = (dhidden * up_act * sigmoid * (1.0 + gate_act * (1.0 - sigmoid))).astype(BF16)
    d_up = (dhidden * silu).astype(BF16)

    coefs = factor * mm_t(nexts, normed)
    next_gate = 0.5 * (gate_all[tokens:] - low_rank(coefs, d_gate))
    next_up = 0.5 * (up_all[tokens:] - low_rank(coefs, d_up))
    to_mate = jnp.stack((next_gate[tokens:], next_up[tokens:])).astype(BF16)
    from_mate = passed_along(to_mate, partner_offset).astype(F32)

    dterm = (mm_t(d_gate, gate) + mm_t(d_up, up)).astype(BF16)
    term = mm(hidden, down)
    own = lax.dynamic_slice_in_dim(term, position * rows, rows, 0) + values
    term = lax.dynamic_update_slice_in_dim(term, own, position * rows, 0).astype(BF16)
    slot_terms = mm(select, term).astype(BF16).reshape(-1, replicas, rows, features)

    gate_next = next_gate[:tokens] + from_mate[0]
    up_next = next_up[:tokens] + from_mate[1]
    hidden_own = (jax.nn.silu(gate_next) * up_next).astype(BF16)
    hidden_mate = passed_along(hidden_own, partner_offset)
    hidden_both = jnp.concatenate((hidden_own, hidden_mate), 0)
    down_coefs = factor * mm_t(hidden_both, hidden)
    term_next = (0.5 * (mm(hidden_both, down) - low_rank(down_coefs, cotangent))).astype(BF16)
    term_next = term_next.reshape(2, replicas, rows, features)
    slots, dnormed, own_sum = sum_terms(
        term_next[1], slot_terms, dterm.reshape(replicas, rows, features), term_next[0]
    )
    next_out = (own_sum + next_values).astype(BF16)
    forwarded = slots.reshape(slot_rows, features)
    scaled = gain[None, :] * dnormed
    cotangent_own = lax.dynamic_slice_in_dim(cotangent, position * rows, rows, 0)
    input_grad = (
        cotangent_own.astype(F32)
        + row_scale * scaled
        - values * row_scale**3 * jnp.mean(values * scaled, axis=1, keepdims=True)
    ).astype(BF16)
    return (forwarded[None], input_grad[None], next_out[None])


def solution(mesh):
    in_specs = (
        P("section", "rep", None),
        P("section", "rep", None),
        P("section", "rep", None),
        P("section", None),
        P("section", None, "rep"),
        P("section", None, "rep"),
        P("section", "rep", None),
        P("section", None, None),
    )
    out_specs = (P("section", "rep", None), P("section", "rep", None), P("section", "rep", None))
    return jax.shard_map(
        per_device, mesh=mesh, in_specs=in_specs, out_specs=out_specs, check_vma=False
    )
```

```python
import functools

import jax
import jax.numpy as jnp
from jax import lax
from jax.experimental import pallas as pl
from jax.experimental.pallas import tpu as pltpu
from jax.sharding import PartitionSpec as P

BLK = 2
epsilon = 1e-05
step_rate = 0.5
F32 = jnp.float32
BF16 = jnp.bfloat16


QUARTERS = 4
CORES = 2
DEPTH_Z = 4


def place(ny):
    me = lax.axis_index("rep")

    def index(z, y, core):
        return (z * ny + y) * CORES + core

    return me // (CORES * ny), (me // CORES) % ny, me % CORES, index


def greet(ny, z, y, core, index, across=()):
    barrier = pltpu.get_barrier_semaphore()
    peers = [{"rep": index((z + d) % DEPTH_Z, y, core)} for d in range(1, DEPTH_Z)]
    peers += [{"rep": index(z, (y + d) % ny, core)} for d in range(1, ny)]
    peers += [{"rep": index(z, y, 1 - core)}]
    peers += [{"section": section} for section in across]
    for peer in peers:
        pl.semaphore_signal(
            barrier, inc=1, device_id=peer, device_id_type=pl.DeviceIdType.MESH
        )
    pl.semaphore_wait(barrier, len(peers))


def remote(src, dst, send, recv, peer):
    return pltpu.make_async_remote_copy(
        src_ref=src,
        dst_ref=dst,
        send_sem=send,
        recv_sem=recv,
        device_id=peer if isinstance(peer, dict) else {"rep": peer},
        device_id_type=pl.DeviceIdType.MESH,
    )


def routing_matrices(counts, rows, blocks_dev, capacity, groups):
    replicas = counts.shape[0]
    tokens = replicas * rows

    def iota(shape, axis):
        return lax.broadcasted_iota(jnp.int32, shape, axis)

    square = (replicas, replicas)
    counts = counts.astype(F32)
    ahead = (iota(square, 0) < iota(square, 1)).astype(F32)
    behind = (iota(square, 1) < iota(square, 0)).astype(F32)
    row_start = mm(counts, ahead)
    column_start = mm(behind, counts)
    receiver = iota(square, 1).astype(F32)
    raw = tokens * QUARTERS
    spread = jnp.ones((replicas, raw), F32)
    spread_down = jnp.ones((groups * tokens, replicas), F32)
    target = (iota((tokens, raw), 0) % BLK).astype(F32)
    target_down = (iota((groups * tokens, tokens), 1) % BLK).astype(F32)
    owner = iota((tokens, replicas), 0) // rows == iota((tokens, replicas), 1)
    block = iota((tokens, replicas), 0) % rows // BLK
    for b in range(blocks_dev):
        inside = (row_start <= b) & (row_start + counts > b)
        slot = jnp.where(inside, receiver * capacity + column_start + b - row_start, 0.0)
        rows_of = (owner & (block == b)).astype(F32)
        target = target + BLK * mm(rows_of, mm(slot, spread))
        target_down = target_down + BLK * mm_t(mm_t(spread_down, slot), rows_of)
    lane = iota((tokens, raw), 1)
    quarter = lane % (QUARTERS * rows) // rows
    slot_row = lane // (QUARTERS * rows) * (rows * groups) + lane % rows
    picks = [
        [
            ((target == (slot_row + g * rows).astype(F32)) & (quarter == q)).astype(F32)
            for g in range(groups)
        ]
        for q in range(QUARTERS)
    ]
    line = iota((groups * tokens, tokens), 0)
    inner = line % tokens
    sent = inner // rows * (rows * groups) + line // tokens * rows + inner % rows
    own = iota((tokens, raw), 0)
    own = own // rows * (QUARTERS * rows) + own % rows
    compact = [(lane == own + q * rows).astype(F32) for q in range(QUARTERS)]
    return picks, compact, (target_down == sent.astype(F32)).astype(F32)


def gather_kernel(
    ny, rows, blocks_dev, head_ref, back_ref, wiring_ref, lhs, cotangent, select,
    head, back, mates, send, send_x, recv
):
    z, y, core, index = place(ny)
    sections = lax.axis_size("section")
    section = lax.axis_index("section")
    mate = (section + sections // 2) % sections
    following = (section + 1) % sections
    before = (section + sections - 1) % sections
    greet(ny, z, y, core, index, (mate, following, before))
    me = index(z, y, core)
    sibling = index(z, y, 1 - core)
    outs = (head, back, mates)
    width = mates.shape[2]

    def hop(kind, way, shard, peer):
        out = outs[kind].at[shard]
        return remote(out, out, send.at[kind, way, shard], recv.at[kind, shard], peer)

    def over_x(shard):
        return remote(
            head.at[shard, :, pl.ds(width, width)],
            mates.at[shard],
            send_x.at[shard],
            recv.at[2, shard],
            {"section": mate},
        )

    def arrive(kind, shard):
        hop(kind, 0, shard, sibling).wait_recv()

    back_copy = remote(
        back_ref, back.at[me], send_x.at[send_x.shape[0] - 1], recv.at[1, me], {"section": before}
    )
    head[me] = head_ref[...]
    back_copy.start()

    def arrivals(d):
        for step in (1, -1) if d else (0,):
            yield step, z - step * d, (z - step * d >= 0) & (z - step * d < DEPTH_Z)

    def onward(kind, d, step, zz, act):
        shard = index(zz, y, core)
        for way, to in enumerate((1, -1)):
            if step in (0, to):

                @pl.when((z + to >= 0) & (z + to < DEPTH_Z))
                def _():
                    act(hop(kind, way, shard, index(z + to, y, core)))

        for dy in range(1, ny):
            act(hop(kind, 2 + dy, shard, index(z, (y + dy) % ny, core)))
        act(hop(kind, 2, shard, sibling))
        if kind == 0:
            act(over_x(shard))

    def along_z(d):
        for kind in range(2):
            for step, zz, there in arrivals(d):

                @pl.when(there)
                def _():
                    if d or kind:
                        arrive(kind, index(zz, y, core))
                    onward(kind, d, step, zz, lambda copy: copy.start())

    def from_y(d):
        for kind in range(2):
            for step, zz, there in arrivals(d):

                @pl.when(there)
                def _():
                    for dy in range(1, ny):
                        shard = index(zz, (y + dy) % ny, core)
                        arrive(kind, shard)
                        hop(kind, 2, shard, sibling).start()
                        if kind == 0:
                            over_x(shard).start()

    along_z(0)
    tokens = cotangent.shape[0]
    groups = back.shape[2] // width
    picks, compact, sent = routing_matrices(
        wiring_ref[...], rows, blocks_dev, groups * rows // BLK, groups
    )
    select[...] = sent.astype(BF16)
    for d in range(1, DEPTH_Z):
        along_z(d)
        from_y(d - 1)
    from_y(DEPTH_Z - 1)
    every = [(dz, dy) for dy in range(ny) for dz in range(DEPTH_Z)]
    for dz, dy in every:
        shard = index((z + dz) % DEPTH_Z, (y + dy) % ny, core)
        arrive(2, shard)
        hop(2, 2, shard, sibling).start()
    for kind in range(3):
        for dz, dy in every:
            arrive(kind, index((z + dz) % DEPTH_Z, (y + dy) % ny, 1 - core))
    flat = [out[...].reshape(tokens * QUARTERS, out.shape[2]) for out in outs]
    for q in range(QUARTERS):
        columns = slice(q * width, (q + 1) * width)
        pick = compact[q].astype(BF16)
        both = mm(pick, flat[0]).astype(BF16)
        lhs[:tokens, columns] = both[:, :width]
        lhs[tokens : 2 * tokens, columns] = both[:, width:]
        lhs[2 * tokens :, columns] = mm(pick, flat[2]).astype(BF16)
        cot = sum(
            mm(picks[q][g].astype(BF16), flat[1][:, g * width : (g + 1) * width])
            for g in range(groups)
        )
        cotangent[:, columns] = cot.astype(BF16)
    back_copy.wait_send()
    for kind in range(2):
        for d in range(DEPTH_Z):
            for step, zz, there in arrivals(d):

                @pl.when(there)
                def _():
                    onward(kind, d, step, zz, lambda copy: copy.wait_send())
                    for dy in range(1, ny):
                        shard = index(zz, (y + dy) % ny, core)
                        hop(kind, 2, shard, sibling).wait_send()
                        if kind == 0:
                            over_x(shard).wait_send()

    for dz, dy in every:
        hop(2, 2, index((z + dz) % DEPTH_Z, (y + dy) % ny, core), sibling).wait_send()


def gather_shards(head, back, wiring, rows, blocks_dev):
    replicas = lax.axis_size("rep")
    ny = replicas // (CORES * DEPTH_Z)
    tokens = replicas * rows
    tall, wide = head.shape
    groups = back.shape[1] // (wide // 2)
    vmem = pl.BlockSpec(memory_space=pltpu.VMEM)
    return pl.pallas_call(
        functools.partial(gather_kernel, ny, rows, blocks_dev),
        out_shape=[
            jax.ShapeDtypeStruct((3 * tokens, QUARTERS * wide // 2), BF16),
            jax.ShapeDtypeStruct((tokens, QUARTERS * wide // 2), BF16),
            jax.ShapeDtypeStruct((groups * tokens, tokens), BF16),
        ],
        in_specs=[vmem] * 3,
        out_specs=[vmem] * 3,
        scratch_shapes=[
            pltpu.VMEM((replicas,) + head.shape, BF16),
            pltpu.VMEM((replicas,) + back.shape, BF16),
            pltpu.VMEM((replicas, tall, wide // 2), BF16),
            pltpu.SemaphoreType.DMA((3, 2 + ny, replicas)),
            pltpu.SemaphoreType.DMA((replicas + 1,)),
            pltpu.SemaphoreType.DMA((3, replicas)),
        ],
        compiler_params=pltpu.CompilerParams(
            collective_id=0, has_side_effects=True, vmem_limit_bytes=32 * 2**20
        ),
    )(head, back, wiring)


def sum_kernel(ny, routed, *refs):
    kinds = routed + 3
    terms = refs[:kinds]
    slots_out, rest_out = refs[kinds : kinds + 2]
    from_core, part, from_y, summed, from_z, to_x, from_x, slot_sum = refs[kinds + 2 : kinds + 10]
    send, recv_core, recv_y, recv_z, recv_x, recv_slot = refs[kinds + 10 :]
    z, y, core, index = place(ny)
    sections = lax.axis_size("section")
    section = lax.axis_index("section")
    mate = (section + sections // 2) % sections
    following = (section + 1) % sections
    before = (section + sections - 1) % sections
    greet(ny, z, y, core, index, (mate, following, before))
    sibling = index(z, y, 1 - core)
    started = []

    def push(src, dst, recv, peer):
        copy = remote(src, dst, send.at[len(started)], recv, peer)
        copy.start()
        started.append(copy)
        return copy

    y_order = list(range(1, ny)) + [0]
    z_order = list(range(2, DEPTH_Z - 1)) + [1, DEPTH_Z - 1, 0]
    core_copies, y_copies, z_copies, totals = {}, {}, {}, {}
    for k in range(kinds):
        for dy in y_order:
            yy = (y + dy) % ny
            core_copies[k, dy] = push(
                terms[k].at[1 - core, yy], from_core.at[k, yy], recv_core.at[k, dy], sibling
            )

    x_copies = {}
    for dy in y_order:
        yy = (y + dy) % ny
        core_copies[0, dy].wait_recv()
        to_x[yy] = (terms[0][core, yy].astype(F32) + from_core[0, yy].astype(F32)).astype(BF16)
        x_copies[dy] = push(to_x.at[yy], from_x.at[yy], recv_x.at[dy], {"section": mate})

    def pair_sum(k, yy, zz=slice(None)):
        total = terms[k][core, yy, zz].astype(F32) + from_core[k, yy, zz].astype(F32)
        if k == kinds - 1:
            total = total + from_x[yy, zz].astype(F32)
        return total

    def to_y(k):
        for dy in y_order[:-1]:
            yy = (y + dy) % ny
            core_copies[k, dy].wait_recv()
            if k == kinds - 1:
                x_copies[dy].wait_recv()
            part[k, dy - 1] = pair_sum(k, yy).astype(BF16)
            y_copies[k, dy] = push(
                part.at[k, dy - 1],
                from_y.at[k, dy - 1],
                recv_y.at[k, dy - 1],
                index(z, yy, core),
            )

    def to_z(k):
        core_copies[k, 0].wait_recv()
        if k == kinds - 1:
            x_copies[0].wait_recv()
        for dy in y_order[:-1]:
            y_copies[k, dy].wait_recv()
        for dz in z_order:
            zz = (z + dz) % DEPTH_Z
            total = pair_sum(k, y, zz)
            for dy in range(1, ny):
                total = total + from_y[k, dy - 1, zz].astype(F32)
            if dz:
                summed[k, dz - 1] = total.astype(BF16)
                z_copies[k, dz] = push(
                    summed.at[k, dz - 1],
                    from_z.at[k, dz - 1],
                    recv_z.at[k, dz - 1],
                    index(zz, y, core),
                )
        totals[k] = total

    slot_copies = []

    def finish(k):
        total = totals[k]
        for dz in z_order[:-1]:
            z_copies[k, dz].wait_recv()
            total = total + from_z[k, dz - 1].astype(F32)
        if k <= routed:
            slot_sum[k - 1] = total.astype(BF16)
            slot_copies.append(
                push(
                    slot_sum.at[k - 1],
                    slots_out.at[k - 1],
                    recv_slot.at[k - 1],
                    {"section": following},
                )
            )
        else:
            rest_out[k - routed - 1] = total

    for k in range(1, kinds + 2):
        if k < kinds:
            to_y(k)
        if 2 <= k <= kinds:
            to_z(k - 1)
        if k >= 3:
            finish(k - 2)
    for copy in slot_copies:
        copy.wait_recv()
    for copy in started:
        copy.wait_send()


def lay_terms(terms):
    replicas, rows, features = terms.shape
    ny = replicas // (CORES * DEPTH_Z)
    width = features // QUARTERS
    laid = terms.reshape(DEPTH_Z, ny, CORES, rows, QUARTERS, width)
    return laid.transpose(2, 1, 0, 4, 3, 5).reshape(CORES, ny, DEPTH_Z, rows * QUARTERS, width)


def lay_back(value, rows):
    tall, width = value.shape[-2:]
    value = value.reshape(-1, QUARTERS, rows, width).transpose(0, 2, 1, 3)
    return value.reshape(-1, rows, QUARTERS * width)


def sum_terms(mate_terms, slot_terms, d_terms, own_terms):
    laid = [lay_terms(v) for v in (mate_terms, *slot_terms, d_terms, own_terms)]
    _, ny, _, tall, width = laid[0].shape
    routed = len(slot_terms)
    kinds = len(laid)
    rows = mate_terms.shape[1]
    copies = kinds * (ny + ny - 1 + DEPTH_Z - 1) + ny + routed
    vmem = pl.BlockSpec(memory_space=pltpu.VMEM)
    slots, rest = pl.pallas_call(
        functools.partial(sum_kernel, ny, routed),
        out_shape=[
            jax.ShapeDtypeStruct((routed, tall, width), BF16),
            jax.ShapeDtypeStruct((2, tall, width), F32),
        ],
        in_specs=[vmem] * kinds,
        out_specs=[vmem] * 2,
        scratch_shapes=[
            pltpu.VMEM((kinds, ny, DEPTH_Z, tall, width), BF16),
            pltpu.VMEM((kinds, ny - 1, DEPTH_Z, tall, width), BF16),
            pltpu.VMEM((kinds, ny - 1, DEPTH_Z, tall, width), BF16),
            pltpu.VMEM((kinds, DEPTH_Z - 1, tall, width), BF16),
            pltpu.VMEM((kinds, DEPTH_Z - 1, tall, width), BF16),
            pltpu.VMEM((ny, DEPTH_Z, tall, width), BF16),
            pltpu.VMEM((ny, DEPTH_Z, tall, width), BF16),
            pltpu.VMEM((routed, tall, width), BF16),
            pltpu.SemaphoreType.DMA((copies,)),
            pltpu.SemaphoreType.DMA((kinds, ny)),
            pltpu.SemaphoreType.DMA((kinds, ny - 1)),
            pltpu.SemaphoreType.DMA((kinds, DEPTH_Z - 1)),
            pltpu.SemaphoreType.DMA((ny,)),
            pltpu.SemaphoreType.DMA((routed,)),
        ],
        compiler_params=pltpu.CompilerParams(
            collective_id=1, has_side_effects=True, vmem_limit_bytes=40 * 2**20
        ),
    )(*laid)
    rest = lay_back(rest, rows)
    return lay_back(slots, rows), rest[0], rest[1]


def passed_along(value, by):
    peers = lax.axis_size("section")
    return lax.ppermute(value, "section", [(i, (i + by) % peers) for i in range(peers)])


def mm(a, b):
    return jnp.dot(a, b, preferred_element_type=F32)


def mm_t(a, b):
    return lax.dot_general(a, b, (((1,), (1,)), ((), ())), preferred_element_type=F32)


def normalize(layer_rows, gain_row):
    values = layer_rows.astype(F32)
    row_scale = lax.rsqrt(jnp.mean(values * values, axis=1, keepdims=True) + epsilon)
    return values, row_scale, (values * row_scale * gain_row[None, :]).astype(BF16)


def low_rank(coefs, factors):
    high = coefs.astype(BF16)
    low = (coefs - high.astype(F32)).astype(BF16)
    return mm(jnp.concatenate((high, low), 1), jnp.concatenate((factors, factors), 0))


def per_device(layer_in, next_in, returned, norm_gain, gate_weight, up_weight, down_weight, wiring):
    replicas = lax.axis_size("rep")
    position = lax.axis_index("rep")
    partner_offset = lax.axis_size("section") // 2
    rows = layer_in.shape[1]
    features = layer_in.shape[2]
    blocks_dev = rows // BLK
    slot_rows = returned.shape[1]
    tokens = rows * replicas
    gain = norm_gain[0]
    gate, up, down = gate_weight[0], up_weight[0], down_weight[0]
    factor = step_rate / tokens

    values, row_scale, normed_own = normalize(layer_in[0], gain)
    next_values, _, next_own = normalize(next_in[0], gain)
    width = features // QUARTERS

    def quartered(value):
        groups = value.reshape(-1, rows, QUARTERS, width).transpose(2, 1, 0, 3)
        return groups.reshape(QUARTERS * rows, -1)

    lhs, cotangent, select = gather_shards(
        quartered(jnp.concatenate((normed_own, next_own), 0)),
        quartered(returned[0]),
        wiring[0],
        rows,
        blocks_dev,
    )
    normed = lhs[:tokens]
    nexts = lhs[tokens:]

    gate_all = mm(lhs, gate)
    up_all = mm(lhs, up)
    gate_act, up_act = gate_all[:tokens], up_all[:tokens]
    sigmoid = jax.nn.sigmoid(gate_act)
    silu = gate_act * sigmoid
    hidden = (silu * up_act).astype(BF16)
    dhidden = mm_t(cotangent, down)
    d_gate = (dhidden * up_act * sigmoid * (1.0 + gate_act * (1.0 - sigmoid))).astype(BF16)
    d_up = (dhidden * silu).astype(BF16)

    coefs = factor * mm_t(nexts, normed)
    next_gate = 0.5 * (gate_all[tokens:] - low_rank(coefs, d_gate))
    next_up = 0.5 * (up_all[tokens:] - low_rank(coefs, d_up))
    to_mate = jnp.stack((next_gate[tokens:], next_up[tokens:])).astype(BF16)
    from_mate = passed_along(to_mate, partner_offset).astype(F32)

    dterm = (mm_t(d_gate, gate) + mm_t(d_up, up)).astype(BF16)
    term = mm(hidden, down)
    own = lax.dynamic_slice_in_dim(term, position * rows, rows, 0) + values
    term = lax.dynamic_update_slice_in_dim(term, own, position * rows, 0).astype(BF16)
    slot_terms = mm(select, term).astype(BF16).reshape(-1, replicas, rows, features)

    gate_next = next_gate[:tokens] + from_mate[0]
    up_next = next_up[:tokens] + from_mate[1]
    hidden_own = (jax.nn.silu(gate_next) * up_next).astype(BF16)
    hidden_mate = passed_along(hidden_own, partner_offset)
    hidden_both = jnp.concatenate((hidden_own, hidden_mate), 0)
    down_coefs = factor * mm_t(hidden_both, hidden)
    term_next = (0.5 * (mm(hidden_both, down) - low_rank(down_coefs, cotangent))).astype(BF16)
    term_next = term_next.reshape(2, replicas, rows, features)
    slots, dnormed, own_sum = sum_terms(
        term_next[1], slot_terms, dterm.reshape(replicas, rows, features), term_next[0]
    )
    next_out = (own_sum + next_values).astype(BF16)
    forwarded = slots.reshape(slot_rows, features)
    scaled = gain[None, :] * dnormed
    cotangent_own = lax.dynamic_slice_in_dim(cotangent, position * rows, rows, 0)
    input_grad = (
        cotangent_own.astype(F32)
        + row_scale * scaled
        - values * row_scale**3 * jnp.mean(values * scaled, axis=1, keepdims=True)
    ).astype(BF16)
    return (forwarded[None], input_grad[None], next_out[None])


def solution(mesh):
    in_specs = (
        P("section", "rep", None),
        P("section", "rep", None),
        P("section", "rep", None),
        P("section", None),
        P("section", None, "rep"),
        P("section", None, "rep"),
        P("section", "rep", None),
        P("section", None, None),
    )
    out_specs = (P("section", "rep", None), P("section", "rep", None), P("section", "rep", None))
    return jax.shard_map(
        per_device, mesh=mesh, in_specs=in_specs, out_specs=out_specs, check_vma=False
    )
```
